128 devices in a mesh: struct: 4 (over x), fluid: 32 (over z, y, core).
Axes of the slice: x: 4, y: 4, z: 4, core: 2. Of those that a mesh axis runs over, the one named last changes fastest.
Arguments:
- shell_motion: float32 [3, 1048576], P(None, ('struct', 'fluid')), may hold values from -6 to 6
- owner: int32 [1048576, 1], P(('struct', 'fluid')), may hold values from 0 to 127; in each aligned block of 8192 rows (0 to 8191, 8192 to 16383, ...) at most 128 rows name the same one
- stencil_slot: int32 [4, 8, 256, 128], P(None, 'struct', 'fluid'), may hold values from 0 to 16383
- stencil_weight: float32 [4, 8, 256, 128], P(None, 'struct', 'fluid'), may hold values from 0 to 0.5
- prev_motion: float32 [3, 8, 256, 256], P(None, 'struct', 'fluid'), may hold values from -6 to 6
- node_offset: float32 [3, 8, 256, 256], P(None, 'struct', 'fluid'), may hold values from -0.07 to 0.07
- cell_split: int32 [8, 256, 256], P('struct', 'fluid'), may hold values from 0 to 3
Outputs:
- mesh_motion: float32 [3, 8, 256, 256], P(None, 'struct', 'fluid')
The draws below stay inside these ranges and needn't reach their ends.
Inputs may be any that keep to these rules, and one draw needn't show every extreme that they name: Among the 8192 shell nodes of one device, no owner is named by more than 128 of them, a bound that some block reaches.
All inputs are finite; a program needn't handle non-finite values.
Results may differ from the reference program's by a relative error of at most 0.0003.
Values sent between devices are 32-bit elements; how exact they have to be, the bound alone decides.
No kernel may reach another device: no remote copies, remote signals or barrier semaphores. Data moves between devices by JAX's collectives and lax.ppermute only.
A program may use at most 64 MiB of HBM per device.

```python
import math
from functools import partial
from functools import reduce
import jax
import jax.numpy as jnp
import numpy as np
from jax import lax

CY = 2
CZ = 8
NX = 256
IF_DEV = 8192
WALL = 128
STENCIL = 4
SWEEPS = 4
NY = 8
NZ = 256
NIF = 1048576
CAP = 128
SLOTS = 16384
N_STRUCT = 4
N_FLUID = 32
DEVICES = 128


def with_ends(values, key, smallest, high):
    extent = values.shape
    place = [jax.random.randint(jax.random.fold_in(key, axis), (), 0, extent[axis]) for axis in range(len(extent))]
    values = values.at[tuple(place)].set(smallest)
    longest = extent.index(max(extent))
    place[longest] = (place[longest] + 1) % extent[longest]
    return values.at[tuple(place)].set(high)


def shard_levels(own_key, extent, shards, smallest, largest):
    def one(axis_at, blocks):
        heights = jax.random.uniform(jax.random.fold_in(jax.random.fold_in(own_key, 6), axis_at), (blocks,), jnp.float32, smallest / len(shards), largest / len(shards))
        return jnp.repeat(jnp.exp(heights), extent[axis_at] // blocks).reshape((-1,) + (1,) * (len(extent) - axis_at - 1))

    factor_of = one(*shards[0])
    for cut in shards[1:]:
        factor_of = factor_of * one(*cut)
    return factor_of


def deal_out(key, own, number, rows, amount, top, reach, lean):
    ranking = jax.random.permutation(key, amount)
    heavy_load, usual = load_shares(amount, rows * top, reach, lean, True), load_shares(amount, rows * top, reach, lean, False)
    places = jnp.arange(amount)

    def named(sizes, turn):
        used = int((sizes > 0).sum())
        fixed = max(1, used // 4)
        passed = fixed + (places - fixed + turn * (used - fixed)) % max(1, amount - fixed)
        return jnp.zeros((amount,), jnp.int32).at[ranking[jnp.where(places < fixed, places, passed)]].set(jnp.asarray(sizes, jnp.int32))

    sizes = jnp.where(number % 4 == 0, named(heavy_load, number // 4), named(usual, number - number // 4 - 1))
    mixed = jax.random.permutation(jax.random.fold_in(own, 3), amount)
    giver, receiver = mixed[0:amount // 2 * 2:2], mixed[1:amount // 2 * 2:2]
    room = jnp.minimum(sizes[giver] - 1, reach - sizes[receiver]) // 2
    room = jnp.where((giver == ranking[0]) | (receiver == ranking[0]) | (sizes[receiver] == 0), 0, jnp.maximum(room, 0))
    passed = jax.random.randint(jax.random.fold_in(own, 4), (amount // 2,), 0, 1 << 20) % (room + 1)
    sizes = sizes.at[giver].add(-passed).at[receiver].add(passed)
    items = jnp.searchsorted(jnp.cumsum(sizes), jnp.arange(rows * top), side="right").astype(jnp.int32)
    table = items.reshape(top, rows).T
    table = table[jax.random.permutation(jax.random.fold_in(own, 1), rows)]
    turn = jax.random.randint(jax.random.fold_in(own, 2), (rows, 1), 0, top)
    return jnp.take_along_axis(table, (jnp.arange(top)[None, :] + turn) % top, axis=1)


def load_shares(count, total, limit, slope, full):
    loads = [(1 << 20) // math.isqrt(standing ** slope) + 1 for standing in range(1, count + 1)]
    largest = limit if full else min(limit, max(-(-total // count), total * loads[0] // sum(loads)))
    least = 1 if total - largest >= count - 1 else 0
    given, surplus = [largest] + [least] * (count - 1), total - largest - least * (count - 1)
    while surplus > 0:
        free = [i for i in range(1, count) if given[i] < largest] or [i for i in range(1, count) if given[i] < limit]
        pool, left = sum([loads[i] for i in free]), surplus
        for i in free:
            more = min(limit - given[i], max(1, left * loads[i] // pool), surplus)
            given[i] = given[i] + more
            surplus = surplus - more
    return np.array(given)


def normal_values(stream_key, dims, deviation, most, cuts=(), kind=jnp.bfloat16):
    gain = shard_levels(stream_key, dims, cuts, -0.22, 0.18) if cuts else 1.0
    array = jax.random.normal(stream_key, dims, jnp.float32) * deviation * gain
    return jnp.minimum(jnp.maximum(array, -most), most).astype(kind)


def setup_inputs(seed: int = 0) -> dict:
    key_of = jax.random.split(jax.random.key(seed), 8)
    shell_motion = normal_values(key_of[0], (3, NIF), 1.0, 6.0, ((1, 128),), jnp.float32)
    owner_keys = jax.random.split(jax.random.fold_in(key_of[1], 1), NIF // IF_DEV)
    owner_turns = jax.random.permutation(jax.random.fold_in(key_of[1], 3), NIF // IF_DEV)
    owner = jax.vmap(lambda own, number: deal_out(jax.random.fold_in(key_of[1], 2), own, number, IF_DEV, DEVICES, 1, CAP, 2))(owner_keys, owner_turns).reshape((NIF, 1))
    stencil_slot = with_ends(jax.random.randint(key_of[2], (STENCIL, NY, NZ, WALL), 0, SLOTS), jax.random.fold_in(key_of[2], 1), 0, SLOTS - 1).astype(jnp.int32)
    stencil_weight = jnp.clip(0.5 * jax.random.uniform(key_of[3], (STENCIL, NY, NZ, WALL), jnp.float32) ** shard_levels(key_of[3], (STENCIL, NY, NZ, WALL), ((1, 4), (2, 32)), -0.2, 0.2), 0.0, 0.5)
    prev_motion = normal_values(key_of[4], (3, NY, NZ, NX), 1.0, 6.0, ((1, 4), (2, 32)), jnp.float32)
    node_offset = jnp.clip(jax.random.uniform(key_of[5], (3, NY, NZ, NX), jnp.float32, -0.07, 0.07) * shard_levels(key_of[5], (3, NY, NZ, NX), ((1, 4), (2, 32)), -0.4, 0.0), -0.07, 0.07)
    cell_split = with_ends(jax.random.randint(key_of[6], (NY, NZ, NX), 0, 4), jax.random.fold_in(key_of[6], 1), 0, 3).astype(jnp.int32)
    return dict(shell_motion=shell_motion, owner=owner, stencil_slot=stencil_slot, stencil_weight=stencil_weight, prev_motion=prev_motion, node_offset=node_offset, cell_split=cell_split)


LAMBDA_RATIO = 1.0
RELAX_FACTOR = 0.5
STEP_ORDERS = ((0, 1, 2), (0, 2, 1), (1, 0, 2), (1, 2, 0), (2, 0, 1), (2, 1, 0))
CORNER_LIST = tuple((shift_x, shift_y, shift_z) for shift_x in (0, 1) for shift_y in (0, 1) for shift_z in (0, 1))


def cross_product(left_vec, right_vec):
    return jnp.stack([left_vec[1] * right_vec[2] - left_vec[2] * right_vec[1],
                      left_vec[2] * right_vec[0] - left_vec[0] * right_vec[2],
                      left_vec[0] * right_vec[1] - left_vec[1] * right_vec[0]])


def select_flip(flip_y, flip_z, unflipped, flipped_z, flipped_y, flipped_both):
    return jnp.where(flip_y, jnp.where(flip_z, flipped_both, flipped_y), jnp.where(flip_z, flipped_z, unflipped))


def reflect_corners(corners, flip_y, flip_z):
    result = {}
    for corner in CORNER_LIST:
        shift_x, shift_y, shift_z = corner
        result[corner] = select_flip(flip_y, flip_z, corners[corner], corners[(shift_x, shift_y, 1 - shift_z)],
                                     corners[(shift_x, 1 - shift_y, shift_z)], corners[(shift_x, 1 - shift_y, 1 - shift_z)])
    return result


def flip_masks(split_codes):
    flip_y = (split_codes // 2) == 1
    flip_z = (split_codes % 2) == 1
    sign_y = jnp.where(flip_y, -1.0, 1.0).astype(jnp.float32)
    sign_z = jnp.where(flip_z, -1.0, 1.0).astype(jnp.float32)
    return flip_y, flip_z, sign_y, sign_z


def lattice_edge(vertex, sign_y, sign_z):
    return jnp.stack([jnp.full_like(sign_y, float(vertex[0])), sign_y * vertex[1], sign_z * vertex[2]])


def element_gradients(offsets, step_order, sign_y, sign_z):
    position = [0, 0, 0]
    vertex_path = [(0, 0, 0)]
    for axis_id in step_order:
        position[axis_id] = 1
        vertex_path.append(tuple(position))
    anchor = offsets[vertex_path[0]]
    edge_list = [lattice_edge(vertex, sign_y, sign_z) + offsets[vertex] - anchor for vertex in vertex_path[1:]]
    across_one = cross_product(edge_list[1], edge_list[2])
    across_two = cross_product(edge_list[2], edge_list[0])
    across_three = cross_product(edge_list[0], edge_list[1])
    volume_six = jnp.sum(edge_list[0] * across_one, axis=0)
    grad_one = across_one / volume_six
    grad_two = across_two / volume_six
    grad_three = across_three / volume_six
    grad_zero = -(grad_one + grad_two + grad_three)
    return vertex_path, [grad_zero, grad_one, grad_two, grad_three]


def element_forces(offsets, displace, sign_y, sign_z):
    forces = {corner: jnp.zeros_like(displace[corner]) for corner in CORNER_LIST}
    for step_order in STEP_ORDERS:
        vertex_path, gradient_list = element_gradients(offsets, step_order, sign_y, sign_z)
        tensor = displace[vertex_path[0]][:, None] * gradient_list[0][None, :]
        for vertex in range(1, 4):
            tensor = tensor + displace[vertex_path[vertex]][:, None] * gradient_list[vertex][None, :]
        trace_sum = tensor[0, 0] + tensor[1, 1] + tensor[2, 2]
        symmetric = tensor + jnp.swapaxes(tensor, 0, 1)
        for vertex in range(4):
            gradient = gradient_list[vertex]
            nodal_force = LAMBDA_RATIO * trace_sum * gradient + jnp.sum(symmetric * gradient[None, :], axis=1)
            forces[vertex_path[vertex]] = forces[vertex_path[vertex]] + nodal_force
    return forces


def element_diagonal(offsets, sign_y, sign_z):
    result = {corner: jnp.zeros_like(offsets[corner]) for corner in CORNER_LIST}
    for step_order in STEP_ORDERS:
        vertex_path, gradient_list = element_gradients(offsets, step_order, sign_y, sign_z)
        for vertex in range(4):
            gradient = gradient_list[vertex]
            entry = (LAMBDA_RATIO + 1.0) * gradient * gradient + jnp.sum(gradient * gradient, axis=0)
            result[vertex_path[vertex]] = result[vertex_path[vertex]] + entry
    return result


def row_corners(lower, upper):
    return {corner: jnp.roll(upper if corner[1] else lower, (-corner[2], -corner[0]), axis=(-2, -1)) for corner in CORNER_LIST}


def row_assemble(per_corner):
    lower_part = reduce(jnp.add, [jnp.roll(per_corner[corner], (corner[2], corner[0]), axis=(-2, -1)) for corner in CORNER_LIST if corner[1] == 0])
    upper_part = reduce(jnp.add, [jnp.roll(per_corner[corner], (corner[2], corner[0]), axis=(-2, -1)) for corner in CORNER_LIST if corner[1] == 1])
    return lower_part, upper_part


def combine_rows(pair):
    lower_part, upper_part = pair
    return jnp.transpose(lower_part + jnp.roll(upper_part, 1, axis=0), (1, 0, 2, 3))


def row_slices(nodal_field, row_index):
    lower = lax.dynamic_index_in_dim(nodal_field, row_index, 1, keepdims=False)
    upper = lax.dynamic_index_in_dim(nodal_field, (row_index + 1) % NY, 1, keepdims=False)
    return row_corners(lower, upper)


def row_masks(cell_split, row_index):
    return flip_masks(lax.dynamic_index_in_dim(cell_split, row_index, 0, keepdims=False))


def diagonal_row(node_offset, cell_split, row_index):
    flip_y, flip_z, sign_y, sign_z = row_masks(cell_split, row_index)
    offsets = reflect_corners(row_slices(node_offset, row_index), flip_y, flip_z)
    return row_assemble(reflect_corners(element_diagonal(offsets, sign_y, sign_z), flip_y, flip_z))


def force_row(node_offset, cell_split, current, row_index):
    flip_y, flip_z, sign_y, sign_z = row_masks(cell_split, row_index)
    offsets = reflect_corners(row_slices(node_offset, row_index), flip_y, flip_z)
    displace = reflect_corners(row_slices(current, row_index), flip_y, flip_z)
    return row_assemble(reflect_corners(element_forces(offsets, displace, sign_y, sign_z), flip_y, flip_z))


def reference(shell_motion, owner, stencil_slot, stencil_weight, prev_motion, node_offset, cell_split):
    devices = N_STRUCT * N_FLUID
    slot_count = devices * CAP
    targets = jnp.arange(devices, dtype=jnp.int32)

    def pack_source(source):
        owner_rows = lax.dynamic_slice_in_dim(owner[:, 0], source * IF_DEV, IF_DEV)
        values = lax.dynamic_slice_in_dim(shell_motion, source * IF_DEV, IF_DEV, 1)
        onehot = (owner_rows[:, None] == targets[None, :]).astype(jnp.int32)
        before = jnp.cumsum(onehot, axis=0) - onehot
        slot_rank = jnp.sum(before * onehot, axis=1)
        slot_place = (owner_rows * CAP + slot_rank).astype(jnp.int32)
        return jnp.zeros((3, slot_count), dtype=shell_motion.dtype).at[:, slot_place].set(values)

    packed = lax.map(pack_source, targets)
    received = packed.reshape(devices, 3, devices, CAP).transpose(1, 2, 0, 3).reshape(3, devices * slot_count)
    row_owner = (jnp.arange(NY, dtype=jnp.int32) // CY) * N_FLUID
    column_owner = jnp.arange(NZ, dtype=jnp.int32) // CZ
    holder = row_owner[:, None] + column_owner[None, :]
    flat_index = (holder[None, :, :, None] * slot_count + stencil_slot).astype(jnp.int32)
    gathered = jnp.take(received, flat_index.reshape(-1), axis=1).reshape(3, STENCIL, NY, NZ, WALL)
    wall_values = jnp.sum(stencil_weight[None] * gathered, axis=1)
    motion = jnp.concatenate([wall_values, prev_motion[:, :, :, WALL:]], axis=3)
    is_wall = (jnp.arange(NX, dtype=jnp.int32) < WALL)[None, None, None, :]
    rows_index = jnp.arange(NY, dtype=jnp.int32)
    diagonal = combine_rows(lax.map(partial(diagonal_row, node_offset, cell_split), rows_index))
    for sweep_index in range(SWEEPS):
        forces = combine_rows(lax.map(partial(force_row, node_offset, cell_split, motion), rows_index))
        motion = jnp.where(is_wall, motion, motion - RELAX_FACTOR * forces / diagonal)
    return motion
```

```python
import jax
import jax.numpy as jnp
from jax import lax
from jax.experimental import pallas as pl
from jax.experimental.pallas import tpu as pltpu
from jax.sharding import PartitionSpec as P

SWEEPS = 4
RELAX_FACTOR = 0.5
STEP_ORDERS = ((0, 1, 2), (0, 2, 1), (1, 0, 2), (1, 2, 0), (2, 0, 1), (2, 1, 0))
BITS = (0, 1)
CORNERS = tuple((a, b, c) for a in BITS for b in BITS for c in BITS)
STEPS = tuple(
    (x, y, z) for z in (-1, 0, 1) for y in (-1, 0, 1) for x in (-1, 0, 1) if (x, y, z) != (0, 0, 0)
)
SLOT_OF = {step: k for k, step in enumerate(STEPS)}
SELF = len(STEPS)
ENTRY = ((0, 3, 4), (3, 1, 5), (4, 5, 2))
BOTH = ("struct", "fluid")
DEPTH = SWEEPS
F32, BF16, I32 = jnp.float32, jnp.bfloat16, jnp.int32
VMEM = pl.BlockSpec(memory_space=pltpu.VMEM)


def params(mebibytes):
    return pltpu.CompilerParams(vmem_limit_bytes=mebibytes * 2**20)


def pack_kernel(owner_ref, value_ref, out_ref, left_ref, right_ref):
    count = owner_ref.shape[1]
    width = 256
    rows = lax.broadcasted_iota(I32, (width, width + 128), 0)
    columns = lax.broadcasted_iota(I32, (width, width + 128), 1)
    earlier = jnp.where((rows < columns) | (columns >= width), 1.0, 0.0).astype(BF16)
    owners = lax.broadcasted_iota(I32, (128, width), 0)
    pairs = lax.broadcasted_iota(I32, (64, width), 0)
    places = lax.broadcasted_iota(I32, (256, width), 0)
    base = jnp.zeros((128, 128), F32)
    for k in range(count // width):
        part = pl.ds(k * width, width)
        own = owner_ref[:, part]
        hit = owners == own
        before = jnp.dot(
            jnp.where(hit, 1.0, 0.0).astype(BF16), earlier, preferred_element_type=F32
        )
        running = before[:, :width] + jnp.concatenate([base, base], axis=1)
        rank = jnp.sum(jnp.where(hit, running, 0.0), axis=0, keepdims=True).astype(I32)
        base = base + before[:, width:]
        right_ref[:, part] = jnp.where(places == (own & 1) * 128 + rank, 1.0, 0.0).astype(BF16)
        half = pairs == (own >> 1)
        for c in range(3):
            value = value_ref[c : c + 1, part]
            high = value.astype(BF16).astype(F32)
            low = value - high
            left_ref[c * 64 : c * 64 + 64, part] = jnp.where(half, high, 0.0).astype(BF16)
            left_ref[192 + c * 64 : 256 + c * 64, part] = jnp.where(half, low, 0.0).astype(BF16)
    product = lax.dot_general(
        left_ref[...], right_ref[...], (((1,), (1,)), ((), ())), preferred_element_type=F32
    )
    both = product[:192] + product[192:]
    for c in range(3):
        for h in range(2):
            out_ref[pl.ds(h, 64, stride=2), c, :] = both[c * 64 : c * 64 + 64, h * 128 : h * 128 + 128]


def pack(owner, shell_motion):
    count = shell_motion.shape[1]
    return pl.pallas_call(
        pack_kernel,
        out_shape=jax.ShapeDtypeStruct((128, 3, 128), F32),
        in_specs=[VMEM] * 2,
        out_specs=VMEM,
        scratch_shapes=[pltpu.VMEM((384, count), BF16), pltpu.VMEM((256, count), BF16)],
        compiler_params=params(24),
        name="pack",
    )(owner.reshape(1, count), shell_motion)


def gather_kernel(received_ref, slot_ref, weight_ref, out_ref, table_ref):
    for c in range(3):
        flat = received_ref[:, c, :].T
        high = flat.astype(BF16).astype(F32)
        low = flat - high
        for part, base in ((high, 0), (low, 192)):
            at = base + c * 64
            table_ref[at : at + 64, :128] = part[:64].astype(BF16)
            table_ref[at : at + 64, 128:] = part[64:].astype(BF16)
    table = table_ref[...]
    picks = lax.broadcasted_iota(I32, (256, 256), 0)
    places = lax.broadcasted_iota(I32, (64, 256), 0)
    for y in range(2):
        for z in range(0, 8, 2):
            total = [jnp.zeros((64, 256), F32) for _ in range(3)]
            for t in range(4):
                slot = jnp.concatenate([slot_ref[t, y, z + k : z + k + 1, :] for k in BITS], axis=1)
                weight = jnp.concatenate([weight_ref[t, y, z + k : z + k + 1, :] for k in BITS], axis=1)
                pick = ((slot >> 6) & 1) * 128 + (slot >> 7)
                hot = jnp.where(picks == pick, 1.0, 0.0).astype(BF16)
                found = jnp.dot(table, hot, preferred_element_type=F32)
                share = jnp.where(places == (slot & 63), weight, 0.0)
                for c in range(3):
                    at = c * 64
                    total[c] = total[c] + share * (found[at : at + 64] + found[at + 192 : at + 256])
            for c in range(3):
                line = jnp.sum(total[c], axis=0, keepdims=True)
                for k in BITS:
                    out_ref[c, y, z + k : z + k + 1, :] = line[:, k * 128 : k * 128 + 128]


def gather(received, stencil_slot, stencil_weight):
    return pl.pallas_call(
        gather_kernel,
        out_shape=jax.ShapeDtypeStruct((3, 2, 8, 128), F32),
        in_specs=[VMEM] * 3,
        out_specs=VMEM,
        scratch_shapes=[pltpu.VMEM((384, 256), BF16)],
        compiler_params=params(16),
        name="gather",
    )(received, stencil_slot, stencil_weight)


def cross(u, v):
    return [
        u[1] * v[2] - u[2] * v[1],
        u[2] * v[0] - u[0] * v[2],
        u[0] * v[1] - u[1] * v[0],
    ]


def cell_blocks(corner, code):
    flip_y = code >= 2
    flip_z = (code == 1) | (code == 3)
    sign_y = jnp.where(flip_y, -1.0, 1.0)
    sign_z = jnp.where(flip_z, -1.0, 1.0)
    named = {}
    for a, b, c in CORNERS:
        named[a, b, c] = [jnp.where(flip_y, corner[a, 1 - b, c][p], corner[a, b, c][p]) for p in range(3)]
    named = {
        (a, b, c): [jnp.where(flip_z, named[a, b, 1 - c][p], named[a, b, c][p]) for p in range(3)]
        for a, b, c in CORNERS
    }
    edge = {}
    for v in CORNERS[1:]:
        moved = [named[v][p] - named[0, 0, 0][p] for p in range(3)]
        if v[0]:
            moved[0] = moved[0] + 1.0
        if v[1]:
            moved[1] = moved[1] + sign_y
        if v[2]:
            moved[2] = moved[2] + sign_z
        edge[v] = moved
    top = (1, 1, 1)
    over = {v: cross(edge[v], edge[top]) for v in CORNERS[1:-1]}
    blocks = {}
    for order in STEP_ORDERS:
        at = [0, 0, 0]
        path = [(0, 0, 0)]
        for axis in order:
            at[axis] = 1
            path.append(tuple(at))
        one, two = path[1], path[2]
        across = [over[two], [-w for w in over[one]], cross(edge[one], edge[two])]
        volume = sum(edge[one][p] * over[two][p] for p in range(3))
        inverse = 1.0 / volume
        grad = [None] + [[w * inverse for w in across[m]] for m in range(3)]
        grad[0] = [-(grad[1][p] + grad[2][p] + grad[3][p]) for p in range(3)]
        for i in range(4):
            for j in range(i + 1, 4):
                g, h = grad[i], grad[j]
                same = [g[p] * h[p] for p in range(3)]
                trace = same[0] + same[1] + same[2]
                block = [same[p] + same[p] + trace for p in range(3)]
                block += [g[p] * h[q] + g[q] * h[p] for p, q in ((0, 1), (0, 2), (1, 2))]
                key = (path[i], path[j])
                blocks[key] = [o + n for o, n in zip(blocks[key], block)] if key in blocks else block

    def pick(mask, yes, no):
        return [jnp.where(mask, y, n) for y, n in zip(yes, no)]

    def keep(mask, values):
        return [jnp.where(mask, v, 0.0) for v in values]

    along_x = {(b, c): blocks[(0, b, c), (1, b, c)] for b in BITS for c in BITS}
    along_x = {(b, c): pick(flip_y, along_x[1 - b, c], along_x[b, c]) for b, c in along_x}
    along_x = {(b, c): pick(flip_z, along_x[b, 1 - c], along_x[b, c]) for b, c in along_x}
    along_y = {(a, c): blocks[(a, 0, c), (a, 1, c)] for a in BITS for c in BITS}
    along_y = {(a, c): pick(flip_z, along_y[a, 1 - c], along_y[a, c]) for a, c in along_y}
    along_z = {(a, b): blocks[(a, b, 0), (a, b, 1)] for a in BITS for b in BITS}
    along_z = {(a, b): pick(flip_y, along_z[a, 1 - b], along_z[a, b]) for a, b in along_z}
    no_y, no_z, unlike = ~flip_y, ~flip_z, flip_y ^ flip_z
    in_xy = [blocks[(0, 0, c), (1, 1, c)] for c in BITS]
    in_xy = [pick(flip_z, in_xy[1 - c], in_xy[c]) for c in BITS]
    in_xz = [blocks[(0, b, 0), (1, b, 1)] for b in BITS]
    in_xz = [pick(flip_y, in_xz[1 - b], in_xz[b]) for b in BITS]
    in_yz = [blocks[(a, 0, 0), (a, 1, 1)] for a in BITS]
    body = blocks[(0, 0, 0), top]
    return dict(
        x=along_x,
        y=along_y,
        z=along_z,
        xy=[(keep(no_y, v), keep(flip_y, v)) for v in in_xy],
        xz=[(keep(no_z, v), keep(flip_z, v)) for v in in_xz],
        yz=[(keep(~unlike, v), keep(unlike, v)) for v in in_yz],
        xyz={
            (0, 0): keep(no_y & no_z, body),
            (0, 1): keep(no_y & flip_z, body),
            (1, 0): keep(flip_y & no_z, body),
            (1, 1): keep(flip_y & flip_z, body),
        },
    )


def fill_rows(target_ref, rows_refs, odd, channel, to, lanes):
    own, swap1, swap2, swap3 = rows_refs
    for r in range(2):
        one, three = swap1[channel, r, :, lanes], swap3[channel, r, :, lanes]
        for place, value in (
            (0, own[channel, r, :, lanes]),
            (2, jnp.where(odd, three, one)),
            (4, swap2[channel, r, :, lanes]),
            (6, jnp.where(odd, one, three)),
        ):
            target_ref[to, :, place + r, :] = value


def assemble_kernel(odd_ref, own_ref, swap1_ref, swap2_ref, swap3_ref, coef_ref, step_ref, field_ref):
    odd = odd_ref[0] == 1
    for c in range(4):
        fill_rows(field_ref, (own_ref, swap1_ref, swap2_ref, swap3_ref), odd, c, c, slice(None))
    planes = field_ref.shape[1]

    def back_y(values):
        return [pltpu.roll(v, 1, 0) for v in values]

    def back_x(values):
        return [pltpu.roll(v, 1, 1) for v in values]

    def plus(u, v):
        return [p + q for p, q in zip(u, v)]

    def put(plane, step, values):
        for e in range(6):
            coef_ref[plane, SLOT_OF[step], e] = values[e][:, 128:]

    def add(plane, step, values):
        for e in range(6):
            at = SLOT_OF[step]
            coef_ref[plane, at, e] = coef_ref[plane, at, e] + values[e][:, 128:]

    def cells(k, _):
        corner = {}
        for c in BITS:
            for p in range(3):
                low = field_ref[p, k + c]
                up = pltpu.roll(low, 7, 0)
                for b, row in ((0, low), (1, up)):
                    corner.setdefault((0, b, c), []).append(row)
                    corner.setdefault((1, b, c), []).append(pltpu.roll(row, 255, 1))
        kinds = cell_blocks(corner, field_ref[3, k])
        low, high = k, k + 1
        z = kinds["z"]
        both = [plus(z[a, 0], back_y(z[a, 1])) for a in BITS]
        s = plus(both[0], back_x(both[1]))
        put(low, (0, 0, 1), s)
        put(high, (0, 0, -1), s)
        (up0, down0), (up1, down1) = kinds["xz"]
        s = plus(up0, back_y(up1))
        put(low, (1, 0, 1), s)
        put(high, (-1, 0, -1), back_x(s))
        s = plus(down0, back_y(down1))
        put(high, (1, 0, -1), s)
        put(low, (-1, 0, 1), back_x(s))
        (up0, down0), (up1, down1) = kinds["yz"]
        s = plus(up0, back_x(up1))
        put(low, (0, 1, 1), s)
        put(high, (0, -1, -1), back_y(s))
        s = plus(down0, back_x(down1))
        put(high, (0, 1, -1), s)
        put(low, (0, -1, 1), back_y(s))
        body = kinds["xyz"]
        put(low, (1, 1, 1), body[0, 0])
        put(high, (-1, -1, -1), back_x(back_y(body[0, 0])))
        put(high, (1, 1, -1), body[0, 1])
        put(low, (-1, -1, 1), back_x(back_y(body[0, 1])))
        put(low, (1, -1, 1), back_y(body[1, 0]))
        put(high, (-1, 1, -1), back_x(body[1, 0]))
        put(high, (1, -1, -1), back_y(body[1, 1]))
        put(low, (-1, 1, 1), back_x(body[1, 1]))
        for c, plane, store in ((0, low, add), (1, high, put)):
            s = plus(kinds["x"][0, c], back_y(kinds["x"][1, c]))
            store(plane, (1, 0, 0), s)
            store(plane, (-1, 0, 0), back_x(s))
            s = plus(kinds["y"][0, c], back_x(kinds["y"][1, c]))
            store(plane, (0, 1, 0), s)
            store(plane, (0, -1, 0), back_y(s))
            up, down = kinds["xy"][c]
            store(plane, (1, 1, 0), up)
            store(plane, (-1, -1, 0), back_x(back_y(up)))
            store(plane, (1, -1, 0), back_y(down))
            store(plane, (-1, 1, 0), back_x(down))
        return 0

    lax.fori_loop(0, planes - 1, cells, 0)

    def selves(k, _):
        for e in range(6):
            total = coef_ref[k, 0, e]
            for m in range(1, SELF):
                total = total + coef_ref[k, m, e]
            coef_ref[k, SELF, e] = -total
            if e < 3:
                step_ref[k, e] = -RELAX_FACTOR / total
        return 0

    lax.fori_loop(1, planes - 1, selves, 0)


def assemble(odd, rows):
    planes = rows[0].shape[2]
    return pl.pallas_call(
        assemble_kernel,
        out_shape=(
            jax.ShapeDtypeStruct((planes, SELF + 1, 6, 8, 128), F32),
            jax.ShapeDtypeStruct((planes, 3, 8, 128), F32),
        ),
        in_specs=[pl.BlockSpec(memory_space=pltpu.SMEM)] + [VMEM] * 4,
        out_specs=(VMEM, VMEM),
        scratch_shapes=[pltpu.VMEM((4, planes, 8, 256), F32)],
        compiler_params=params(30),
        cost_estimate=pl.CostEstimate(flops=200000000, bytes_accessed=12000000, transcendentals=0),
        name="assemble",
    )(odd, *rows)


def sweep_kernel(odd_ref, *refs):
    prev_rows, wall_rows = refs[:4], refs[4:8]
    coef_ref, step_ref, wall_ref, out_ref, motion_ref, edge_ref, near_ref = refs[8:]
    odd = odd_ref[0] == 1
    planes = motion_ref.shape[1]
    for c in range(3):
        fill_rows(motion_ref, prev_rows, odd, c + 4, c, slice(128, 256))
        fill_rows(edge_ref, wall_rows, odd, c, c, slice(None))
    lane = lax.broadcasted_iota(I32, (8, 128), 1)
    first, last = lane == 0, lane == 127

    def neighbours(k, _):
        for c in range(3):
            here = motion_ref[c, k]
            side = edge_ref[c, k]
            for x, value in (
                (-1, jnp.where(first, pltpu.roll(side, 1, 1), pltpu.roll(here, 1, 1))),
                (0, here),
                (1, jnp.where(last, pltpu.roll(side, 127, 1), pltpu.roll(here, 127, 1))),
            ):
                near_ref[k, c, 1, x + 1] = value
                near_ref[k, c, 0, x + 1] = pltpu.roll(value, 1, 0)
                near_ref[k, c, 2, x + 1] = pltpu.roll(value, 7, 0)
        return 0

    def relax(k, _):
        force = [None] * 3
        for m, (x, y, z) in enumerate(STEPS + ((0, 0, 0),)):
            block = [coef_ref[k, m, e] for e in range(6)]
            other = [near_ref[k + z, c, y + 1, x + 1] for c in range(3)]
            for p in range(3):
                term = sum(block[ENTRY[p][q]] * other[q] for q in range(3))
                force[p] = term if force[p] is None else force[p] + term
        for p in range(3):
            motion_ref[p, k] = motion_ref[p, k] - step_ref[k, p] * force[p]
        return 0

    for sweep in range(SWEEPS):
        lax.fori_loop(sweep, planes - sweep, neighbours, 0)
        lax.fori_loop(sweep + 1, planes - sweep - 1, relax, 0)
    for c in range(3):
        for y in range(2):
            out_ref[c, y, :, :128] = wall_ref[c, y]
            out_ref[c, y, :, 128:] = motion_ref[c, DEPTH : planes - DEPTH, y, :]


def sweeps(odd, rows, wall_rows, coef, step, wall):
    planes = rows[0].shape[2]
    return pl.pallas_call(
        sweep_kernel,
        out_shape=jax.ShapeDtypeStruct((3, 2, planes - 2 * DEPTH, 256), F32),
        in_specs=[pl.BlockSpec(memory_space=pltpu.SMEM)] + [VMEM] * 11,
        out_specs=VMEM,
        scratch_shapes=[
            pltpu.VMEM((3, planes, 8, 128), F32),
            pltpu.VMEM((3, planes, 8, 128), F32),
            pltpu.VMEM((planes, 3, 3, 3, 8, 128), F32),
        ],
        compiler_params=params(30),
        name="sweeps",
    )(odd, *rows, *wall_rows, coef, step, wall)


def swap(block, partner):
    struct_count, fluid_count = lax.axis_size("struct"), lax.axis_size("fluid")
    route = []
    for s in range(struct_count):
        for f in range(fluid_count):
            to_s, to_f = partner(s, f)
            route.append((s * fluid_count + f, to_s * fluid_count + to_f % fluid_count))
    return lax.ppermute(block, BOTH, route)


def widen(block, even):
    count = block.shape[2]
    first, last = block[:, :, :DEPTH], block[:, :, count - DEPTH :]
    in_pair = swap(jnp.where(even, last, first), lambda s, f: (s, f ^ 1))
    next_pair = swap(jnp.where(even, first, last), lambda s, f: (s, ((f - 1) ^ 1) + 1))
    before = jnp.where(even, next_pair, in_pair)
    after = jnp.where(even, in_pair, next_pair)
    return jnp.concatenate([before, block, after], axis=2)


def all_rows(block):
    return [block] + [swap(block, lambda s, f, m=m: (s ^ m, f)) for m in (1, 2, 3)]


def shards(shell_motion, owner, stencil_slot, stencil_weight, prev_motion, node_offset, cell_split):
    odd = (lax.axis_index("struct") % 2).astype(I32).reshape(1)
    even = lax.axis_index("fluid") % 2 == 0
    packed = pack(owner, shell_motion)
    fields = jnp.concatenate([node_offset, cell_split.astype(F32)[None], prev_motion])
    rows = all_rows(widen(fields, even))
    received = lax.all_to_all(packed, BOTH, split_axis=0, concat_axis=0, tiled=True)
    coef, step = assemble(odd, rows)
    wall = gather(received, stencil_slot, stencil_weight)
    wall_rows = all_rows(widen(wall, even))
    return sweeps(odd, rows, wall_rows, coef, step, wall)


def solution(mesh):
    return jax.shard_map(
        shards,
        mesh=mesh,
        in_specs=(
            P(None, BOTH),
            P(BOTH, None),
            P(None, "struct", "fluid", None),
            P(None, "struct", "fluid", None),
            P(None, "struct", "fluid", None),
            P(None, "struct", "fluid", None),
            P("struct", "fluid", None),
        ),
        out_specs=P(None, "struct", "fluid", None),
        check_vma=False,
    )
```

```python
from functools import partial

import jax
import jax.numpy as jnp
from jax import lax
from jax.experimental import pallas as pl
from jax.experimental.pallas import tpu as pltpu
from jax.sharding import PartitionSpec as P

SWEEPS = 4
RELAX_FACTOR = 0.5
STEP_ORDERS = ((0, 1, 2), (0, 2, 1), (1, 0, 2), (1, 2, 0), (2, 0, 1), (2, 1, 0))
BITS = (0, 1)
CORNERS = tuple((a, b, c) for a in BITS for b in BITS for c in BITS)
STEPS = tuple(
    (x, y, z) for z in (-1, 0, 1) for y in (-1, 0, 1) for x in (-1, 0, 1) if (x, y, z) != (0, 0, 0)
)
SLOT_OF = {step: k for k, step in enumerate(STEPS)}
SELF = len(STEPS)
ENTRY = ((0, 3, 4), (3, 1, 5), (4, 5, 2))
BOTH = ("struct", "fluid")
DEPTH = SWEEPS
SETUP_FLOPS, PLANE_FLOPS = 20000000, 20000000
FULL = 63
F32, BF16, I32 = jnp.float32, jnp.bfloat16, jnp.int32
VMEM = pl.BlockSpec(memory_space=pltpu.VMEM)
SMEM = pl.BlockSpec(memory_space=pltpu.SMEM)
HBM = pl.BlockSpec(memory_space=pltpu.HBM)


def fetch(sources, targets, semaphores):
    copies = [
        pltpu.make_async_copy(source, target, semaphores.at[k])
        for k, (source, target) in enumerate(zip(sources, targets))
    ]
    for copy in copies:
        copy.start()
    for copy in copies:
        copy.wait()


def params(mebibytes):
    return pltpu.CompilerParams(vmem_limit_bytes=int(mebibytes * 2**20))


def pack_kernel(owner_hbm, value_hbm, out_ref, left_ref, right_ref, owner_ref, value_ref, semaphores):
    fetch((owner_hbm, value_hbm), (owner_ref, value_ref), semaphores)
    count = owner_ref.shape[1]
    width = 256
    rows = lax.broadcasted_iota(I32, (width, width + 128), 0)
    columns = lax.broadcasted_iota(I32, (width, width + 128), 1)
    earlier = jnp.where((rows < columns) | (columns >= width), 1.0, 0.0).astype(BF16)
    owners = lax.broadcasted_iota(I32, (128, width), 0)
    pairs = lax.broadcasted_iota(I32, (64, width), 0)
    places = lax.broadcasted_iota(I32, (256, width), 0)
    base = jnp.zeros((128, 128), F32)
    for k in range(count // width):
        part = pl.ds(k * width, width)
        own = owner_ref[:, part]
        hit = owners == own
        before = jnp.dot(
            jnp.where(hit, 1.0, 0.0).astype(BF16), earlier, preferred_element_type=F32
        )
        running = before[:, :width] + jnp.concatenate([base, base], axis=1)
        rank = jnp.sum(jnp.where(hit, running, 0.0), axis=0, keepdims=True).astype(I32)
        base = base + before[:, width:]
        right_ref[:, part] = jnp.where(places == (own & 1) * 128 + rank, 1.0, 0.0).astype(BF16)
        half = pairs == (own >> 1)
        for c in range(3):
            value = value_ref[c : c + 1, part]
            high = value.astype(BF16).astype(F32)
            low = value - high
            left_ref[c * 64 : c * 64 + 64, part] = jnp.where(half, high, 0.0).astype(BF16)
            left_ref[192 + c * 64 : 256 + c * 64, part] = jnp.where(half, low, 0.0).astype(BF16)
    product = lax.dot_general(
        left_ref[...], right_ref[...], (((1,), (1,)), ((), ())), preferred_element_type=F32
    )
    both = product[:192] + product[192:]
    for c in range(3):
        for h in range(2):
            out_ref[pl.ds(h, 64, stride=2), c, :] = both[c * 64 : c * 64 + 64, h * 128 : h * 128 + 128]


def pack(owner, shell_motion):
    count = shell_motion.shape[1]
    return pl.pallas_call(
        pack_kernel,
        out_shape=jax.ShapeDtypeStruct((128, 3, 128), F32),
        in_specs=[HBM] * 2,
        out_specs=VMEM,
        scratch_shapes=[
            pltpu.VMEM((384, count), BF16),
            pltpu.VMEM((256, count), BF16),
            pltpu.VMEM((1, count), I32),
            pltpu.VMEM((3, count), F32),
            pltpu.SemaphoreType.DMA((2,)),
        ],
        compiler_params=params(FULL),
        name="pack",
    )(owner.reshape(1, count), shell_motion)


def payload(channels):
    return (
        jax.ShapeDtypeStruct((channels, 2, 8, 128), F32),
        jax.ShapeDtypeStruct((channels, 2, DEPTH, 128), F32),
        jax.ShapeDtypeStruct((channels, 2, DEPTH, 128), F32),
    )


def emit(refs, even, channel, y, value):
    whole_ref, pair_ref, next_ref = refs
    first, last = value[:DEPTH], value[DEPTH:]
    whole_ref[channel, y] = value
    pair_ref[channel, y] = jnp.where(even, last, first)
    next_ref[channel, y] = jnp.where(even, first, last)


def fields_kernel(even_ref, offset_hbm, split_hbm, prev_hbm, slot_hbm, weight_hbm, *refs):
    out_refs, (slot_ref, weight_ref, offset_ref, split_ref, prev_ref, semaphores) = refs[:3], refs[3:]
    fetch(
        (offset_hbm, split_hbm, prev_hbm, slot_hbm, weight_hbm),
        (offset_ref, split_ref, prev_ref, slot_ref, weight_ref),
        semaphores,
    )
    even = even_ref[0] == 1
    lane = lax.broadcasted_iota(I32, (8, 128), 1)
    for y in range(2):
        code = split_ref[y].astype(F32)
        columns = jnp.where(lane == 3, pltpu.roll(code[:, :128], 4, 1), 0.0)
        for p in range(3):
            wall, free = offset_ref[p, y, :, :128], offset_ref[p, y, :, 128:]
            columns = jnp.where(lane == p, pltpu.roll(wall, p + 1, 1), columns)
            columns = jnp.where(lane == 4 + p, pltpu.roll(free, 4 + p, 1), columns)
            columns = jnp.where(lane == 125 + p, pltpu.roll(wall, 125 + p, 1), columns)
            emit(out_refs, even, p, y, free)
            emit(out_refs, even, 5 + p, y, prev_ref[p, y, :, 128:])
        emit(out_refs, even, 3, y, code[:, 128:])
        emit(out_refs, even, 4, y, columns)


def fields(even, node_offset, cell_split, prev_motion, stencil_slot, stencil_weight):
    return pl.pallas_call(
        fields_kernel,
        out_shape=(
            *payload(8),
            jax.ShapeDtypeStruct(stencil_slot.shape, I32),
            jax.ShapeDtypeStruct(stencil_weight.shape, F32),
        ),
        in_specs=[SMEM] + [HBM] * 5,
        out_specs=(VMEM,) * 5,
        scratch_shapes=[
            pltpu.VMEM(node_offset.shape, F32),
            pltpu.VMEM(cell_split.shape, I32),
            pltpu.VMEM(prev_motion.shape, F32),
            pltpu.SemaphoreType.DMA((5,)),
        ],
        compiler_params=params(FULL),
        name="fields",
    )(even, node_offset, cell_split, prev_motion, stencil_slot, stencil_weight)


def gather_kernel(even_ref, received_ref, slot_ref, weight_ref, out_ref, *more_refs):
    column_refs, table_ref = more_refs[:3], more_refs[3]
    for c in range(3):
        flat = received_ref[:, c, :].T
        high = flat.astype(BF16).astype(F32)
        low = flat - high
        for part, base in ((high, 0), (low, 192)):
            at = base + c * 64
            table_ref[at : at + 64, :128] = part[:64].astype(BF16)
            table_ref[at : at + 64, 128:] = part[64:].astype(BF16)
    table = table_ref[...]
    picks = lax.broadcasted_iota(I32, (256, 256), 0)
    places = lax.broadcasted_iota(I32, (64, 256), 0)
    for y in range(2):
        for z in range(0, 8, 2):
            total = [jnp.zeros((64, 256), F32) for _ in range(3)]
            for t in range(4):
                slot = jnp.concatenate([slot_ref[t, y, z + k : z + k + 1, :] for k in BITS], axis=1)
                weight = jnp.concatenate([weight_ref[t, y, z + k : z + k + 1, :] for k in BITS], axis=1)
                pick = ((slot >> 6) & 1) * 128 + (slot >> 7)
                hot = jnp.where(picks == pick, 1.0, 0.0).astype(BF16)
                found = jnp.dot(table, hot, preferred_element_type=F32)
                share = jnp.where(places == (slot & 63), weight, 0.0)
                for c in range(3):
                    at = c * 64
                    total[c] = total[c] + share * (found[at : at + 64] + found[at + 192 : at + 256])
            for c in range(3):
                line = jnp.sum(total[c], axis=0, keepdims=True)
                for k in BITS:
                    out_ref[c, y, z + k : z + k + 1, :] = line[:, k * 128 : k * 128 + 128]
    lane = lax.broadcasted_iota(I32, (8, 128), 1)
    for y in range(2):
        columns = jnp.zeros((8, 128), F32)
        for c in range(3):
            wall = out_ref[c, y]
            columns = jnp.where(lane == c, pltpu.roll(wall, c + 1, 1), columns)
            columns = jnp.where(lane == 125 + c, pltpu.roll(wall, 125 + c, 1), columns)
        emit(column_refs, even_ref[0] == 1, 0, y, columns)


def gather(even, received, stencil_slot, stencil_weight):
    return pl.pallas_call(
        gather_kernel,
        out_shape=(jax.ShapeDtypeStruct((3, 2, 8, 128), F32), *payload(1)),
        in_specs=[SMEM] + [VMEM] * 3,
        out_specs=(VMEM,) * 4,
        scratch_shapes=[pltpu.VMEM((384, 256), BF16)],
        compiler_params=params(16),
        name="gather",
    )(even, received, stencil_slot, stencil_weight)


def cross(u, v):
    return [
        u[1] * v[2] - u[2] * v[1],
        u[2] * v[0] - u[0] * v[2],
        u[0] * v[1] - u[1] * v[0],
    ]


def cell_blocks(corner, code):
    flip_y = code >= 2
    flip_z = (code == 1) | (code == 3)
    sign_y = jnp.where(flip_y, -1.0, 1.0)
    sign_z = jnp.where(flip_z, -1.0, 1.0)
    named = {}
    for a, b, c in CORNERS:
        named[a, b, c] = [jnp.where(flip_y, corner[a, 1 - b, c][p], corner[a, b, c][p]) for p in range(3)]
    named = {
        (a, b, c): [jnp.where(flip_z, named[a, b, 1 - c][p], named[a, b, c][p]) for p in range(3)]
        for a, b, c in CORNERS
    }
    edge = {}
    for v in CORNERS[1:]:
        moved = [named[v][p] - named[0, 0, 0][p] for p in range(3)]
        if v[0]:
            moved[0] = moved[0] + 1.0
        if v[1]:
            moved[1] = moved[1] + sign_y
        if v[2]:
            moved[2] = moved[2] + sign_z
        edge[v] = moved
    top = (1, 1, 1)
    over = {v: cross(edge[v], edge[top]) for v in CORNERS[1:-1]}
    blocks = {}
    for order in STEP_ORDERS:
        at = [0, 0, 0]
        path = [(0, 0, 0)]
        for axis in order:
            at[axis] = 1
            path.append(tuple(at))
        one, two = path[1], path[2]
        across = [over[two], [-w for w in over[one]], cross(edge[one], edge[two])]
        volume = sum(edge[one][p] * over[two][p] for p in range(3))
        inverse = 1.0 / volume
        grad = [None] + [[w * inverse for w in across[m]] for m in range(3)]
        grad[0] = [-(grad[1][p] + grad[2][p] + grad[3][p]) for p in range(3)]
        for i in range(4):
            for j in range(i + 1, 4):
                g, h = grad[i], grad[j]
                same = [g[p] * h[p] for p in range(3)]
                trace = same[0] + same[1] + same[2]
                block = [same[p] + same[p] + trace for p in range(3)]
                block += [g[p] * h[q] + g[q] * h[p] for p, q in ((0, 1), (0, 2), (1, 2))]
                key = (path[i], path[j])
                blocks[key] = [o + n for o, n in zip(blocks[key], block)] if key in blocks else block

    def pick(mask, yes, no):
        return [jnp.where(mask, y, n) for y, n in zip(yes, no)]

    def keep(mask, values):
        return [jnp.where(mask, v, 0.0) for v in values]

    along_x = {(b, c): blocks[(0, b, c), (1, b, c)] for b in BITS for c in BITS}
    along_x = {(b, c): pick(flip_y, along_x[1 - b, c], along_x[b, c]) for b, c in along_x}
    along_x = {(b, c): pick(flip_z, along_x[b, 1 - c], along_x[b, c]) for b, c in along_x}
    along_y = {(a, c): blocks[(a, 0, c), (a, 1, c)] for a in BITS for c in BITS}
    along_y = {(a, c): pick(flip_z, along_y[a, 1 - c], along_y[a, c]) for a, c in along_y}
    along_z = {(a, b): blocks[(a, b, 0), (a, b, 1)] for a in BITS for b in BITS}
    along_z = {(a, b): pick(flip_y, along_z[a, 1 - b], along_z[a, b]) for a, b in along_z}
    no_y, no_z, unlike = ~flip_y, ~flip_z, flip_y ^ flip_z
    in_xy = [blocks[(0, 0, c), (1, 1, c)] for c in BITS]
    in_xy = [pick(flip_z, in_xy[1 - c], in_xy[c]) for c in BITS]
    in_xz = [blocks[(0, b, 0), (1, b, 1)] for b in BITS]
    in_xz = [pick(flip_y, in_xz[1 - b], in_xz[b]) for b in BITS]
    in_yz = [blocks[(a, 0, 0), (a, 1, 1)] for a in BITS]
    body = blocks[(0, 0, 0), top]
    return dict(
        x=along_x,
        y=along_y,
        z=along_z,
        xy=[(keep(no_y, v), keep(flip_y, v)) for v in in_xy],
        xz=[(keep(no_z, v), keep(flip_z, v)) for v in in_xz],
        yz=[(keep(~unlike, v), keep(unlike, v)) for v in in_yz],
        xyz={
            (0, 0): keep(no_y & no_z, body),
            (0, 1): keep(no_y & flip_z, body),
            (1, 0): keep(flip_y & no_z, body),
            (1, 1): keep(flip_y & flip_z, body),
        },
    )


def fill_rows(target_ref, rows_refs, odd, channel, to):
    own, swap1, swap2, swap3 = rows_refs
    for r in range(2):
        one, three = swap1[channel, r], swap3[channel, r]
        for place, value in (
            (0, own[channel, r]),
            (2, jnp.where(odd, three, one)),
            (4, swap2[channel, r]),
            (6, jnp.where(odd, one, three)),
        ):
            target_ref[to, :, place + r, :] = value


def back_y(values):
    return [pltpu.roll(v, 1, 0) for v in values]


def plus(u, v):
    return [p + q for p, q in zip(u, v)]


MOVING = ("z", "xz_up", "xz_down", "yz_up", "yz_down", "b00", "b01", "b10", "b11") + tuple(
    (name, c) for c in BITS for name in ("x", "y", "up", "down")
)


def node_parts(kinds):
    x, y, z = kinds["x"], kinds["y"], kinds["z"]
    (xz_up0, xz_down0), (xz_up1, xz_down1) = kinds["xz"]
    (yz_up0, yz_down0), (yz_up1, yz_down1) = kinds["yz"]
    body = {key: (v, back_y(v)) for key, v in kinds["xyz"].items()}
    moving = {
        "z": plus(z[1, 0], back_y(z[1, 1])),
        "xz_up": plus(xz_up0, back_y(xz_up1)),
        "xz_down": plus(xz_down0, back_y(xz_down1)),
        "yz_up": yz_up1,
        "yz_down": yz_down1,
        "b00": body[0, 0][1],
        "b01": body[0, 1][1],
        "b10": body[1, 0][0],
        "b11": body[1, 1][0],
    }
    still = {
        "z": plus(z[0, 0], back_y(z[0, 1])),
        "yz_up": yz_up0,
        "yz_down": yz_down0,
        "b00": body[0, 0][0],
        "b01": body[0, 1][0],
        "b10": body[1, 0][1],
        "b11": body[1, 1][1],
    }
    for c in BITS:
        up, down = kinds["xy"][c]
        moving["x", c] = plus(x[0, c], back_y(x[1, c]))
        moving["y", c] = y[1, c]
        moving["up", c] = back_y(up)
        moving["down", c] = down
        still["y", c] = y[0, c]
        still["up", c] = up
        still["down", c] = back_y(down)
    return moving, still


def setup_kernel(odd_ref, own_ref, swap1_ref, swap2_ref, swap3_ref, field_ref, side_ref):
    odd = odd_ref[0] == 1
    for c in range(5):
        fill_rows(field_ref, (own_ref, swap1_ref, swap2_ref, swap3_ref), odd, c, c)
    planes = field_ref.shape[1]
    gap = 128 // planes
    lane = lax.broadcasted_iota(I32, (8, 128), 1)

    packed = jnp.zeros((8, 128), F32)
    for k in range(planes):
        packed = jnp.where(lane // gap == k, pltpu.roll(field_ref[4, k], k * gap, 1), packed)
    corner = {}
    for a in BITS:
        for p in range(3):
            low = pltpu.roll(packed, 128 - (4 * a + p), 1) if a or p else packed
            for c, plane in ((0, low), (1, pltpu.roll(low, 128 - gap, 1))):
                corner.setdefault((a, 0, c), []).append(plane)
                corner.setdefault((a, 1, c), []).append(pltpu.roll(plane, 7, 0))
    moving, _ = node_parts(cell_blocks(corner, pltpu.roll(packed, 125, 1)))
    for m, name in enumerate(MOVING):
        for e in range(6):
            side_ref[m, e] = moving[name][e]


def setup(odd, rows):
    planes = rows[0].shape[2]
    return pl.pallas_call(
        setup_kernel,
        out_shape=(
            jax.ShapeDtypeStruct((5, planes, 8, 128), F32),
            jax.ShapeDtypeStruct((len(MOVING), 6, 8, 128), F32),
        ),
        in_specs=[SMEM] + [VMEM] * 4,
        out_specs=(VMEM,) * 2,
        compiler_params=params(4),
        cost_estimate=pl.CostEstimate(flops=SETUP_FLOPS, bytes_accessed=1000000, transcendentals=0),
        name="setup",
    )(odd, *rows)


def assemble_kernel(start, stop, field_ref, side_ref, coef_ref, step_ref):
    planes = field_ref.shape[1]
    gap = 128 // planes
    lane = lax.broadcasted_iota(I32, (8, 128), 1)
    first, last = lane == 0, lane == 127

    def cells(k, _):
        corner = {}
        for c in BITS:
            edge = field_ref[4, k + c]
            edges = (edge, pltpu.roll(edge, 7, 0))
            for p in range(3):
                low = field_ref[p, k + c]
                for b, row in ((0, low), (1, pltpu.roll(low, 7, 0))):
                    beyond = pltpu.roll(edges[b], 2 - p, 1) if p < 2 else edges[b]
                    corner.setdefault((0, b, c), []).append(row)
                    corner.setdefault((1, b, c), []).append(jnp.where(last, beyond, pltpu.roll(row, 127, 1)))
        moving, still = node_parts(cell_blocks(corner, field_ref[3, k]))
        shift = 128 - k * gap

        def back_x(name):
            m = MOVING.index(name)
            return [
                jnp.where(first, pltpu.roll(side_ref[m, e], shift, 1), pltpu.roll(moving[name][e], 1, 1))
                for e in range(6)
            ]

        def put(plane, step, values):
            for e in range(6):
                coef_ref[plane, SLOT_OF[step], e] = values[e]

        def add(plane, step, values):
            at = SLOT_OF[step]
            for e in range(6):
                coef_ref[plane, at, e] = coef_ref[plane, at, e] + values[e]

        low, high = k - start, k + 1 - start
        s = plus(still["z"], back_x("z"))
        put(low, (0, 0, 1), s)
        put(high, (0, 0, -1), s)
        put(low, (1, 0, 1), moving["xz_up"])
        put(high, (-1, 0, -1), back_x("xz_up"))
        put(high, (1, 0, -1), moving["xz_down"])
        put(low, (-1, 0, 1), back_x("xz_down"))
        s = plus(still["yz_up"], back_x("yz_up"))
        put(low, (0, 1, 1), s)
        put(high, (0, -1, -1), back_y(s))
        s = plus(still["yz_down"], back_x("yz_down"))
        put(high, (0, 1, -1), s)
        put(low, (0, -1, 1), back_y(s))
        put(low, (1, 1, 1), still["b00"])
        put(high, (-1, -1, -1), back_x("b00"))
        put(high, (1, 1, -1), still["b01"])
        put(low, (-1, -1, 1), back_x("b01"))
        put(low, (1, -1, 1), still["b10"])
        put(high, (-1, 1, -1), back_x("b10"))
        put(high, (1, -1, -1), still["b11"])
        put(low, (-1, 1, 1), back_x("b11"))
        for c, plane, store in ((0, low, add), (1, high, put)):
            store(plane, (1, 0, 0), moving["x", c])
            store(plane, (-1, 0, 0), back_x(("x", c)))
            s = plus(still["y", c], back_x(("y", c)))
            store(plane, (0, 1, 0), s)
            store(plane, (0, -1, 0), back_y(s))
            store(plane, (1, 1, 0), still["up", c])
            store(plane, (-1, -1, 0), back_x(("up", c)))
            store(plane, (1, -1, 0), still["down", c])
            store(plane, (-1, 1, 0), back_x(("down", c)))
        return 0

    lax.fori_loop(start, stop, cells, 0)

    def selves(k, _):
        for e in range(6):
            total = coef_ref[k, 0, e]
            for m in range(1, SELF):
                total = total + coef_ref[k, m, e]
            coef_ref[k, SELF, e] = -total
            if e < 3:
                step_ref[k, e] = -RELAX_FACTOR / total
        return 0

    lax.fori_loop(1, stop - start, selves, 0)


def assemble(field, side, start, stop):
    return pl.pallas_call(
        partial(assemble_kernel, start, stop),
        out_shape=(
            jax.ShapeDtypeStruct((stop - start + 1, SELF + 1, 6, 8, 128), F32),
            jax.ShapeDtypeStruct((stop - start + 1, 3, 8, 128), F32),
        ),
        in_specs=[VMEM] * 2,
        out_specs=(VMEM,) * 2,
        compiler_params=params(4),
        cost_estimate=pl.CostEstimate(
            flops=PLANE_FLOPS * (stop - start), bytes_accessed=1000000, transcendentals=0
        ),
        name="assemble",
    )(field, side)


def sweep_kernel(odd_ref, *refs):
    rows_refs = refs[:4]
    coef_a_ref, step_a_ref, coef_b_ref, step_b_ref, wall_ref, out_ref, motion_ref, edge_ref = refs[4:]
    odd = odd_ref[0] == 1
    planes = motion_ref.shape[1]
    middle = planes // 2
    for c in range(3):
        fill_rows(motion_ref, rows_refs, odd, c, c)
    fill_rows(edge_ref, rows_refs, odd, 3, 0)
    lane = lax.broadcasted_iota(I32, (8, 128), 1)
    first, last = lane == 0, lane == 127
    lower = (coef_a_ref, step_a_ref, 0)
    upper = (coef_b_ref, step_b_ref, middle - 1)

    def from_plane(low, parts, k, sums):
        side = edge_ref[0, k]
        near = {}
        for c in range(3):
            here = motion_ref[c, k]
            before = pltpu.roll(side, 128 - c, 1) if c else side
            beyond = pltpu.roll(side, 2 - c, 1) if c < 2 else side
            for x, value in (
                (-1, jnp.where(first, before, pltpu.roll(here, 1, 1))),
                (0, here),
                (1, jnp.where(last, beyond, pltpu.roll(here, 127, 1))),
            ):
                near[c, 0, x] = value
                near[c, -1, x] = pltpu.roll(value, 1, 0)
                near[c, 1, x] = pltpu.roll(value, 7, 0)

        def reach(part, plane, z):
            coef_ref, _, base = part
            force = [None] * 3
            for y in (-1, 0, 1):
                for x in (-1, 0, 1):
                    at = SLOT_OF.get((x, y, z), SELF)
                    block = [coef_ref[plane - base, at, e] for e in range(6)]
                    for p in range(3):
                        term = sum(block[ENTRY[p][q]] * near[q, y, x] for q in range(3))
                        force[p] = term if force[p] is None else force[p] + term
            return force

        to = jnp.maximum(k - 1, 0)
        below = plus(sums[:3], reach(parts[0], to, 1))
        here = plus(sums[3:], reach(parts[1], k, 0))
        above = reach(parts[2], jnp.minimum(k + 1, planes - 1), -1)
        _, step_ref, base = parts[0]

        @pl.when(k > low + 1)
        def _():
            for p in range(3):
                motion_ref[p, to] = motion_ref[p, to] - step_ref[to - base, p] * below[p]

        return tuple(here) + tuple(above)

    def sweep(low, _):
        sums = (jnp.zeros((8, 128), F32),) * 6
        sums = lax.fori_loop(low, middle - 1, partial(from_plane, low, (lower, lower, lower)), sums)
        sums = from_plane(low, (lower, lower, upper), middle - 1, sums)
        sums = from_plane(low, (lower, upper, upper), middle, sums)
        lax.fori_loop(middle + 1, planes - low, partial(from_plane, low, (upper, upper, upper)), sums)
        return 0

    lax.fori_loop(0, SWEEPS, sweep, 0)
    for c in range(3):
        for y in range(2):
            out_ref[c, y, :, :128] = wall_ref[c, y]
            out_ref[c, y, :, 128:] = motion_ref[c, DEPTH : planes - DEPTH, y, :]


def sweeps(odd, rows, lower, upper, wall):
    planes = rows[0].shape[2]
    return pl.pallas_call(
        sweep_kernel,
        out_shape=jax.ShapeDtypeStruct((3, 2, planes - 2 * DEPTH, 256), F32),
        in_specs=[SMEM] + [VMEM] * 9,
        out_specs=VMEM,
        scratch_shapes=[
            pltpu.VMEM((3, planes, 8, 128), F32),
            pltpu.VMEM((1, planes, 8, 128), F32),
        ],
        compiler_params=params(4),
        name="sweeps",
    )(odd, *rows, *lower, *upper, wall)


def swap(block, partner):
    struct_count, fluid_count = lax.axis_size("struct"), lax.axis_size("fluid")
    route = []
    for s in range(struct_count):
        for f in range(fluid_count):
            to_s, to_f = partner(s, f)
            route.append((s * fluid_count + f, to_s * fluid_count + to_f % fluid_count))
    return lax.ppermute(block, BOTH, route)


def planes_apart(parts):
    _, for_pair, for_next = parts
    return (
        swap(for_pair, lambda s, f: (s, f ^ 1)),
        swap(for_next, lambda s, f: (s, ((f - 1) ^ 1) + 1)),
    )


def widen_kernel(even_ref, whole_ref, pair_ref, next_ref, *refs):
    even = even_ref[0] == 1
    channels, _, count, _ = whole_ref.shape
    out_refs, head = refs, 0
    if refs[0].shape[0] + channels == refs[-1].shape[0]:
        head = refs[0].shape[0]
        refs[1][:head] = refs[0][...]
        out_refs = refs[1:]
    for c in range(channels):
        out_ref, to = (out_refs[0], c + head) if c + head < out_refs[0].shape[0] else (out_refs[1], c - out_refs[0].shape[0])
        for y in range(2):
            in_pair, next_pair = pair_ref[c, y], next_ref[c, y]
            out_ref[to, y, :DEPTH] = jnp.where(even, next_pair, in_pair)
            out_ref[to, y, DEPTH : DEPTH + count] = whole_ref[c, y]
            out_ref[to, y, DEPTH + count :] = jnp.where(even, in_pair, next_pair)


def widen(even, parts, channels, head=()):
    _, rows, count, lanes = parts[0].shape
    return pl.pallas_call(
        widen_kernel,
        out_shape=tuple(jax.ShapeDtypeStruct((n, rows, count + 2 * DEPTH, lanes), F32) for n in channels),
        in_specs=[SMEM] + [VMEM] * (3 + len(head)),
        out_specs=(VMEM,) * len(channels),
        compiler_params=params(4),
        name="widen",
    )(even, *parts, *head)


def all_rows(block):
    return [block] + [swap(block, lambda s, f, m=m: (s ^ m, f)) for m in (1, 2, 3)]


def shards(shell_motion, owner, stencil_slot, stencil_weight, prev_motion, node_offset, cell_split):
    odd = (lax.axis_index("struct") & 1).astype(I32).reshape(1)
    even = 1 - (lax.axis_index("fluid") & 1).astype(I32).reshape(1)
    packed = pack(owner, shell_motion)
    *sent, slot, weight = fields(even, node_offset, cell_split, prev_motion, stencil_slot, stencil_weight)
    lattice, prev = widen(even, (sent[0], *planes_apart(sent)), (5, 3))
    field, side = setup(odd, all_rows(lattice))
    received = lax.all_to_all(packed, BOTH, split_axis=0, concat_axis=0, tiled=True)
    received, field, side = lax.optimization_barrier((received, field, side))
    wall, *sent = gather(even, received, slot, weight)
    field, side, *sent = lax.optimization_barrier((field, side, *sent))
    apart = planes_apart(sent)
    lower = assemble(field, side, 0, 8)
    lower, apart = lax.optimization_barrier((lower, apart))
    [joined] = widen(even, (sent[0], *apart), (4,), (prev,))
    field, side, joined = lax.optimization_barrier((field, side, joined))
    rows = all_rows(joined)
    upper = assemble(field, side, 7, 15)
    return sweeps(odd, rows, lower, upper, wall)


def solution(mesh):
    return jax.shard_map(
        shards,
        mesh=mesh,
        in_specs=(
            P(None, BOTH),
            P(BOTH, None),
            P(None, "struct", "fluid", None),
            P(None, "struct", "fluid", None),
            P(None, "struct", "fluid", None),
            P(None, "struct", "fluid", None),
            P("struct", "fluid", None),
        ),
        out_specs=P(None, "struct", "fluid", None),
        check_vma=False,
    )
```

```python
from functools import partial

import jax
import jax.numpy as jnp
from jax import lax
from jax.experimental import pallas as pl
from jax.experimental.pallas import tpu as pltpu
from jax.sharding import PartitionSpec as P

SWEEPS = 4
RELAX_FACTOR = 0.5
STEP_ORDERS = ((0, 1, 2), (0, 2, 1), (1, 0, 2), (1, 2, 0), (2, 0, 1), (2, 1, 0))
BITS = (0, 1)
CORNERS = tuple((a, b, c) for a in BITS for b in BITS for c in BITS)
STEPS = tuple(
    (x, y, z) for z in (-1, 0, 1) for y in (-1, 0, 1) for x in (-1, 0, 1) if (x, y, z) != (0, 0, 0)
)
SLOT_OF = {step: k for k, step in enumerate(STEPS)}
SELF = len(STEPS)
ENTRY = ((0, 3, 4), (3, 1, 5), (4, 5, 2))
BOTH = ("struct", "fluid")
DEPTH = SWEEPS
SETUP_FLOPS, PLANE_FLOPS = 20000000, 20000000
FULL = 63
F32, BF16, I32 = jnp.float32, jnp.bfloat16, jnp.int32
VMEM = pl.BlockSpec(memory_space=pltpu.VMEM)
SMEM = pl.BlockSpec(memory_space=pltpu.SMEM)
HBM = pl.BlockSpec(memory_space=pltpu.HBM)


def fetch(sources, targets, semaphores):
    copies = [
        pltpu.make_async_copy(source, target, semaphores.at[k])
        for k, (source, target) in enumerate(zip(sources, targets))
    ]
    for copy in copies:
        copy.start()
    for copy in copies:
        copy.wait()


def params(mebibytes):
    return pltpu.CompilerParams(vmem_limit_bytes=int(mebibytes * 2**20))


def pack_kernel(owner_hbm, value_hbm, out_ref, left_ref, right_ref, owner_ref, value_ref, semaphores):
    fetch((owner_hbm, value_hbm), (owner_ref, value_ref), semaphores)
    count = owner_ref.shape[1]
    width = 256
    rows = lax.broadcasted_iota(I32, (width, width + 128), 0)
    columns = lax.broadcasted_iota(I32, (width, width + 128), 1)
    earlier = jnp.where((rows < columns) | (columns >= width), 1.0, 0.0).astype(BF16)
    owners = lax.broadcasted_iota(I32, (128, width), 0)
    pairs = lax.broadcasted_iota(I32, (64, width), 0)
    places = lax.broadcasted_iota(I32, (256, width), 0)
    base = jnp.zeros((128, 128), F32)
    for k in range(count // width):
        part = pl.ds(k * width, width)
        own = owner_ref[:, part]
        hit = owners == own
        before = jnp.dot(
            jnp.where(hit, 1.0, 0.0).astype(BF16), earlier, preferred_element_type=F32
        )
        running = before[:, :width] + jnp.concatenate([base, base], axis=1)
        rank = jnp.sum(jnp.where(hit, running, 0.0), axis=0, keepdims=True).astype(I32)
        base = base + before[:, width:]
        right_ref[:, part] = jnp.where(places == (own & 1) * 128 + rank, 1.0, 0.0).astype(BF16)
        half = pairs == (own >> 1)
        for c in range(3):
            value = value_ref[c : c + 1, part]
            high = value.astype(BF16).astype(F32)
            low = value - high
            left_ref[c * 64 : c * 64 + 64, part] = jnp.where(half, high, 0.0).astype(BF16)
            left_ref[192 + c * 64 : 256 + c * 64, part] = jnp.where(half, low, 0.0).astype(BF16)
    product = lax.dot_general(
        left_ref[...], right_ref[...], (((1,), (1,)), ((), ())), preferred_element_type=F32
    )
    both = product[:192] + product[192:]
    for c in range(3):
        for h in range(2):
            out_ref[pl.ds(h, 64, stride=2), c, :] = both[c * 64 : c * 64 + 64, h * 128 : h * 128 + 128]


def pack(owner, shell_motion):
    count = shell_motion.shape[1]
    return pl.pallas_call(
        pack_kernel,
        out_shape=jax.ShapeDtypeStruct((128, 3, 128), F32),
        in_specs=[HBM] * 2,
        out_specs=VMEM,
        scratch_shapes=[
            pltpu.VMEM((384, count), BF16),
            pltpu.VMEM((256, count), BF16),
            pltpu.VMEM((1, count), I32),
            pltpu.VMEM((3, count), F32),
            pltpu.SemaphoreType.DMA((2,)),
        ],
        compiler_params=params(FULL),
        name="pack",
    )(owner.reshape(1, count), shell_motion)


def payload(kept, sent):
    return (
        jax.ShapeDtypeStruct((kept, 2, 8, 128), F32),
        jax.ShapeDtypeStruct((sent, 2, DEPTH, 128), F32),
        jax.ShapeDtypeStruct((sent, 2, DEPTH, 128), F32),
    )


def emit(refs, even, channel, y, value):
    whole_ref, pair_ref, next_ref = refs
    first, last = value[:DEPTH], value[DEPTH:]
    whole_ref[channel, y] = value
    pair_ref[channel, y] = jnp.where(even, last, first)
    next_ref[channel, y] = jnp.where(even, first, last)


def fields_kernel(even_ref, offset_hbm, split_hbm, prev_hbm, slot_hbm, weight_hbm, *refs):
    out_refs, (slot_ref, weight_ref, offset_ref, split_ref, prev_ref, semaphores) = refs[:3], refs[3:]
    fetch(
        (offset_hbm, split_hbm, prev_hbm, slot_hbm, weight_hbm),
        (offset_ref, split_ref, prev_ref, slot_ref, weight_ref),
        semaphores,
    )
    out_refs[0][8:12] = slot_ref[...].astype(F32)
    out_refs[0][12:16] = weight_ref[...]
    even = even_ref[0] == 1
    lane = lax.broadcasted_iota(I32, (8, 128), 1)
    for y in range(2):
        code = split_ref[y].astype(F32)
        columns = jnp.where(lane == 3, pltpu.roll(code[:, :128], 4, 1), 0.0)
        for p in range(3):
            wall, free = offset_ref[p, y, :, :128], offset_ref[p, y, :, 128:]
            columns = jnp.where(lane == p, pltpu.roll(wall, p + 1, 1), columns)
            columns = jnp.where(lane == 4 + p, pltpu.roll(free, 4 + p, 1), columns)
            columns = jnp.where(lane == 125 + p, pltpu.roll(wall, 125 + p, 1), columns)
            emit(out_refs, even, p, y, free)
            emit(out_refs, even, 5 + p, y, prev_ref[p, y, :, 128:])
        emit(out_refs, even, 3, y, code[:, 128:])
        emit(out_refs, even, 4, y, columns)


def fields(even, node_offset, cell_split, prev_motion, stencil_slot, stencil_weight):
    return pl.pallas_call(
        fields_kernel,
        out_shape=payload(16, 8),
        in_specs=[SMEM] + [HBM] * 5,
        out_specs=(VMEM,) * 3,
        scratch_shapes=[
            pltpu.VMEM(stencil_slot.shape, I32),
            pltpu.VMEM(stencil_weight.shape, F32),
            pltpu.VMEM(node_offset.shape, F32),
            pltpu.VMEM(cell_split.shape, I32),
            pltpu.VMEM(prev_motion.shape, F32),
            pltpu.SemaphoreType.DMA((5,)),
        ],
        compiler_params=params(FULL),
        name="fields",
    )(even, node_offset, cell_split, prev_motion, stencil_slot, stencil_weight)


def columns_kernel(even_ref, received_ref, plan_ref, *refs):
    column_refs, table_ref = refs[:3], refs[3]
    for c in range(3):
        flat = received_ref[:, c, :]
        high = flat.astype(BF16).astype(F32)
        low = flat - high
        for part, base in ((high, 0), (low, 192)):
            at = slice(base + c * 64, base + c * 64 + 64)
            table_ref[:128, at] = part[:, :64].astype(BF16)
            table_ref[128:, at] = part[:, 64:].astype(BF16)

    def stacked(first):
        return jnp.concatenate(
            [
                plan_ref[first + t, y, :, x : x + 1]
                for t in range(4)
                for y in range(2)
                for x in (127, 0)
            ]
        )

    slot = stacked(0).astype(I32)
    weight = stacked(4)
    pick = ((slot >> 6) & 1) * 128 + (slot >> 7)
    hot = jnp.where(lax.broadcasted_iota(I32, (128, 256), 1) == pick, 1.0, 0.0).astype(BF16)
    found = jnp.dot(hot, table_ref[...], preferred_element_type=F32)
    found = found[:, :192] + found[:, 192:]
    share = jnp.where(lax.broadcasted_iota(I32, (128, 192), 1) % 64 == (slot & 63), weight, 0.0) * found
    share = share[:32] + share[32:64] + share[64:96] + share[96:]
    values = [jnp.sum(share[:, c * 64 : c * 64 + 64], axis=1, keepdims=True) for c in range(3)]
    lane = lax.broadcasted_iota(I32, (8, 128), 1)
    for y in range(2):
        columns = jnp.zeros((8, 128), F32)
        for c in range(3):
            columns = jnp.where(lane == c, values[c][y * 16 : y * 16 + 8], columns)
            columns = jnp.where(lane == 125 + c, values[c][y * 16 + 8 : y * 16 + 16], columns)
        emit(column_refs, even_ref[0] == 1, 0, y, columns)


def wall_columns(even, received, plan):
    return pl.pallas_call(
        columns_kernel,
        out_shape=payload(1, 1),
        in_specs=[SMEM] + [VMEM] * 2,
        out_specs=(VMEM,) * 3,
        scratch_shapes=[pltpu.VMEM((256, 384), BF16)],
        compiler_params=params(8),
        name="columns",
    )(even, received, plan)


def gather_kernel(received_ref, plan_ref, out_ref, table_ref):
    for c in range(3):
        flat = received_ref[:, c, :].T
        high = flat.astype(BF16).astype(F32)
        low = flat - high
        for part, base in ((high, 0), (low, 192)):
            at = base + c * 64
            table_ref[at : at + 64, :128] = part[:64].astype(BF16)
            table_ref[at : at + 64, 128:] = part[64:].astype(BF16)
    table = table_ref[...]
    picks = lax.broadcasted_iota(I32, (256, 256), 0)
    places = lax.broadcasted_iota(I32, (64, 256), 0)
    for y in range(2):
        for z in range(0, 8, 2):
            total = [jnp.zeros((64, 256), F32) for _ in range(3)]
            for t in range(4):
                slot, weight = [
                    jnp.concatenate([plan_ref[first + t, y, z + k : z + k + 1, :] for k in BITS], axis=1)
                    for first in (0, 4)
                ]
                slot = slot.astype(I32)
                pick = ((slot >> 6) & 1) * 128 + (slot >> 7)
                hot = jnp.where(picks == pick, 1.0, 0.0).astype(BF16)
                found = jnp.dot(table, hot, preferred_element_type=F32)
                share = jnp.where(places == (slot & 63), weight, 0.0)
                for c in range(3):
                    at = c * 64
                    total[c] = total[c] + share * (found[at : at + 64] + found[at + 192 : at + 256])
            for c in range(3):
                line = jnp.sum(total[c], axis=0, keepdims=True)
                for k in BITS:
                    out_ref[c, y, z + k : z + k + 1, :] = line[:, k * 128 : k * 128 + 128]


def gather(received, plan):
    return pl.pallas_call(
        gather_kernel,
        out_shape=jax.ShapeDtypeStruct((3, 2, 8, 128), F32),
        in_specs=[VMEM] * 2,
        out_specs=VMEM,
        scratch_shapes=[pltpu.VMEM((384, 256), BF16)],
        compiler_params=params(8),
        cost_estimate=pl.CostEstimate(flops=60000000, bytes_accessed=1000000, transcendentals=0),
        name="gather",
    )(received, plan)


def cross(u, v):
    return [
        u[1] * v[2] - u[2] * v[1],
        u[2] * v[0] - u[0] * v[2],
        u[0] * v[1] - u[1] * v[0],
    ]


def cell_blocks(corner, code):
    flip_y = code >= 2
    flip_z = (code == 1) | (code == 3)
    sign_y = jnp.where(flip_y, -1.0, 1.0)
    sign_z = jnp.where(flip_z, -1.0, 1.0)
    named = {}
    for a, b, c in CORNERS:
        named[a, b, c] = [jnp.where(flip_y, corner[a, 1 - b, c][p], corner[a, b, c][p]) for p in range(3)]
    named = {
        (a, b, c): [jnp.where(flip_z, named[a, b, 1 - c][p], named[a, b, c][p]) for p in range(3)]
        for a, b, c in CORNERS
    }
    edge = {}
    for v in CORNERS[1:]:
        moved = [named[v][p] - named[0, 0, 0][p] for p in range(3)]
        if v[0]:
            moved[0] = moved[0] + 1.0
        if v[1]:
            moved[1] = moved[1] + sign_y
        if v[2]:
            moved[2] = moved[2] + sign_z
        edge[v] = moved
    top = (1, 1, 1)
    over = {v: cross(edge[v], edge[top]) for v in CORNERS[1:-1]}
    blocks = {}
    for order in STEP_ORDERS:
        at = [0, 0, 0]
        path = [(0, 0, 0)]
        for axis in order:
            at[axis] = 1
            path.append(tuple(at))
        one, two = path[1], path[2]
        across = [over[two], [-w for w in over[one]], cross(edge[one], edge[two])]
        volume = sum(edge[one][p] * over[two][p] for p in range(3))
        inverse = 1.0 / volume
        grad = [None] + [[w * inverse for w in across[m]] for m in range(3)]
        grad[0] = [-(grad[1][p] + grad[2][p] + grad[3][p]) for p in range(3)]
        for i in range(4):
            for j in range(i + 1, 4):
                g, h = grad[i], grad[j]
                same = [g[p] * h[p] for p in range(3)]
                trace = same[0] + same[1] + same[2]
                block = [same[p] + same[p] + trace for p in range(3)]
                block += [g[p] * h[q] + g[q] * h[p] for p, q in ((0, 1), (0, 2), (1, 2))]
                key = (path[i], path[j])
                blocks[key] = [o + n for o, n in zip(blocks[key], block)] if key in blocks else block

    def pick(mask, yes, no):
        return [jnp.where(mask, y, n) for y, n in zip(yes, no)]

    def keep(mask, values):
        return [jnp.where(mask, v, 0.0) for v in values]

    along_x = {(b, c): blocks[(0, b, c), (1, b, c)] for b in BITS for c in BITS}
    along_x = {(b, c): pick(flip_y, along_x[1 - b, c], along_x[b, c]) for b, c in along_x}
    along_x = {(b, c): pick(flip_z, along_x[b, 1 - c], along_x[b, c]) for b, c in along_x}
    along_y = {(a, c): blocks[(a, 0, c), (a, 1, c)] for a in BITS for c in BITS}
    along_y = {(a, c): pick(flip_z, along_y[a, 1 - c], along_y[a, c]) for a, c in along_y}
    along_z = {(a, b): blocks[(a, b, 0), (a, b, 1)] for a in BITS for b in BITS}
    along_z = {(a, b): pick(flip_y, along_z[a, 1 - b], along_z[a, b]) for a, b in along_z}
    no_y, no_z, unlike = ~flip_y, ~flip_z, flip_y ^ flip_z
    in_xy = [blocks[(0, 0, c), (1, 1, c)] for c in BITS]
    in_xy = [pick(flip_z, in_xy[1 - c], in_xy[c]) for c in BITS]
    in_xz = [blocks[(0, b, 0), (1, b, 1)] for b in BITS]
    in_xz = [pick(flip_y, in_xz[1 - b], in_xz[b]) for b in BITS]
    in_yz = [blocks[(a, 0, 0), (a, 1, 1)] for a in BITS]
    body = blocks[(0, 0, 0), top]
    return dict(
        x=along_x,
        y=along_y,
        z=along_z,
        xy=[(keep(no_y, v), keep(flip_y, v)) for v in in_xy],
        xz=[(keep(no_z, v), keep(flip_z, v)) for v in in_xz],
        yz=[(keep(~unlike, v), keep(unlike, v)) for v in in_yz],
        xyz={
            (0, 0): keep(no_y & no_z, body),
            (0, 1): keep(no_y & flip_z, body),
            (1, 0): keep(flip_y & no_z, body),
            (1, 1): keep(flip_y & flip_z, body),
        },
    )


def fill_rows(target_ref, rows_refs, odd, channel, to):
    own, swap1, swap2, swap3 = rows_refs
    for r in range(2):
        one, three = swap1[channel, r], swap3[channel, r]
        for place, value in (
            (0, own[channel, r]),
            (2, jnp.where(odd, three, one)),
            (4, swap2[channel, r]),
            (6, jnp.where(odd, one, three)),
        ):
            target_ref[to, :, place + r, :] = value


def back_y(values):
    return [pltpu.roll(v, 1, 0) for v in values]


def plus(u, v):
    return [p + q for p, q in zip(u, v)]


MOVING = ("z", "xz_up", "xz_down", "yz_up", "yz_down", "b00", "b01", "b10", "b11") + tuple(
    (name, c) for c in BITS for name in ("x", "y", "up", "down")
)


def node_parts(kinds):
    x, y, z = kinds["x"], kinds["y"], kinds["z"]
    (xz_up0, xz_down0), (xz_up1, xz_down1) = kinds["xz"]
    (yz_up0, yz_down0), (yz_up1, yz_down1) = kinds["yz"]
    body = {key: (v, back_y(v)) for key, v in kinds["xyz"].items()}
    moving = {
        "z": plus(z[1, 0], back_y(z[1, 1])),
        "xz_up": plus(xz_up0, back_y(xz_up1)),
        "xz_down": plus(xz_down0, back_y(xz_down1)),
        "yz_up": yz_up1,
        "yz_down": yz_down1,
        "b00": body[0, 0][1],
        "b01": body[0, 1][1],
        "b10": body[1, 0][0],
        "b11": body[1, 1][0],
    }
    still = {
        "z": plus(z[0, 0], back_y(z[0, 1])),
        "yz_up": yz_up0,
        "yz_down": yz_down0,
        "b00": body[0, 0][0],
        "b01": body[0, 1][0],
        "b10": body[1, 0][1],
        "b11": body[1, 1][1],
    }
    for c in BITS:
        up, down = kinds["xy"][c]
        moving["x", c] = plus(x[0, c], back_y(x[1, c]))
        moving["y", c] = y[1, c]
        moving["up", c] = back_y(up)
        moving["down", c] = down
        still["y", c] = y[0, c]
        still["up", c] = up
        still["down", c] = back_y(down)
    return moving, still


def setup_kernel(odd_ref, own_ref, swap1_ref, swap2_ref, swap3_ref, field_ref, side_ref):
    odd = odd_ref[0] == 1
    for c in range(5):
        fill_rows(field_ref, (own_ref, swap1_ref, swap2_ref, swap3_ref), odd, c, c)
    planes = field_ref.shape[1]
    gap = 128 // planes
    lane = lax.broadcasted_iota(I32, (8, 128), 1)

    packed = jnp.zeros((8, 128), F32)
    for k in range(planes):
        packed = jnp.where(lane // gap == k, pltpu.roll(field_ref[4, k], k * gap, 1), packed)
    corner = {}
    for a in BITS:
        for p in range(3):
            low = pltpu.roll(packed, 128 - (4 * a + p), 1) if a or p else packed
            for c, plane in ((0, low), (1, pltpu.roll(low, 128 - gap, 1))):
                corner.setdefault((a, 0, c), []).append(plane)
                corner.setdefault((a, 1, c), []).append(pltpu.roll(plane, 7, 0))
    moving, _ = node_parts(cell_blocks(corner, pltpu.roll(packed, 125, 1)))
    for m, name in enumerate(MOVING):
        for e in range(6):
            side_ref[m, e] = moving[name][e]


def setup(odd, rows):
    planes = rows[0].shape[2]
    return pl.pallas_call(
        setup_kernel,
        out_shape=(
            jax.ShapeDtypeStruct((5, planes, 8, 128), F32),
            jax.ShapeDtypeStruct((len(MOVING), 6, 8, 128), F32),
        ),
        in_specs=[SMEM] + [VMEM] * 4,
        out_specs=(VMEM,) * 2,
        compiler_params=params(4),
        cost_estimate=pl.CostEstimate(flops=SETUP_FLOPS, bytes_accessed=1000000, transcendentals=0),
        name="setup",
    )(odd, *rows)


def assemble_kernel(start, stop, field_ref, side_ref, coef_ref, step_ref):
    planes = field_ref.shape[1]
    gap = 128 // planes
    lane = lax.broadcasted_iota(I32, (8, 128), 1)
    first, last = lane == 0, lane == 127

    def cells(k, _):
        corner = {}
        for c in BITS:
            edge = field_ref[4, k + c]
            edges = (edge, pltpu.roll(edge, 7, 0))
            for p in range(3):
                low = field_ref[p, k + c]
                for b, row in ((0, low), (1, pltpu.roll(low, 7, 0))):
                    beyond = pltpu.roll(edges[b], 2 - p, 1) if p < 2 else edges[b]
                    corner.setdefault((0, b, c), []).append(row)
                    corner.setdefault((1, b, c), []).append(jnp.where(last, beyond, pltpu.roll(row, 127, 1)))
        moving, still = node_parts(cell_blocks(corner, field_ref[3, k]))
        shift = 128 - k * gap

        def back_x(name):
            m = MOVING.index(name)
            return [
                jnp.where(first, pltpu.roll(side_ref[m, e], shift, 1), pltpu.roll(moving[name][e], 1, 1))
                for e in range(6)
            ]

        def put(plane, step, values):
            for e in range(6):
                coef_ref[plane, SLOT_OF[step], e] = values[e]

        def add(plane, step, values):
            at = SLOT_OF[step]
            for e in range(6):
                coef_ref[plane, at, e] = coef_ref[plane, at, e] + values[e]

        low, high = k - start, k + 1 - start
        s = plus(still["z"], back_x("z"))
        put(low, (0, 0, 1), s)
        put(high, (0, 0, -1), s)
        put(low, (1, 0, 1), moving["xz_up"])
        put(high, (-1, 0, -1), back_x("xz_up"))
        put(high, (1, 0, -1), moving["xz_down"])
        put(low, (-1, 0, 1), back_x("xz_down"))
        s = plus(still["yz_up"], back_x("yz_up"))
        put(low, (0, 1, 1), s)
        put(high, (0, -1, -1), back_y(s))
        s = plus(still["yz_down"], back_x("yz_down"))
        put(high, (0, 1, -1), s)
        put(low, (0, -1, 1), back_y(s))
        put(low, (1, 1, 1), still["b00"])
        put(high, (-1, -1, -1), back_x("b00"))
        put(high, (1, 1, -1), still["b01"])
        put(low, (-1, -1, 1), back_x("b01"))
        put(low, (1, -1, 1), still["b10"])
        put(high, (-1, 1, -1), back_x("b10"))
        put(high, (1, -1, -1), still["b11"])
        put(low, (-1, 1, 1), back_x("b11"))
        for c, plane, store in ((0, low, add), (1, high, put)):
            store(plane, (1, 0, 0), moving["x", c])
            store(plane, (-1, 0, 0), back_x(("x", c)))
            s = plus(still["y", c], back_x(("y", c)))
            store(plane, (0, 1, 0), s)
            store(plane, (0, -1, 0), back_y(s))
            store(plane, (1, 1, 0), still["up", c])
            store(plane, (-1, -1, 0), back_x(("up", c)))
            store(plane, (1, -1, 0), still["down", c])
            store(plane, (-1, 1, 0), back_x(("down", c)))
        return 0

    lax.fori_loop(start, stop, cells, 0, unroll=2)

    def selves(k, _):
        for e in range(6):
            total = coef_ref[k, 0, e]
            for m in range(1, SELF):
                total = total + coef_ref[k, m, e]
            coef_ref[k, SELF, e] = -total
            if e < 3:
                step_ref[k, e] = -RELAX_FACTOR / total
        return 0

    lax.fori_loop(1, stop - start, selves, 0, unroll=7)


def assemble(field, side, start, stop):
    return pl.pallas_call(
        partial(assemble_kernel, start, stop),
        out_shape=(
            jax.ShapeDtypeStruct((stop - start + 1, SELF + 1, 6, 8, 128), F32),
            jax.ShapeDtypeStruct((stop - start + 1, 3, 8, 128), F32),
        ),
        in_specs=[VMEM] * 2,
        out_specs=(VMEM,) * 2,
        compiler_params=params(12),
        cost_estimate=pl.CostEstimate(
            flops=PLANE_FLOPS * (stop - start), bytes_accessed=1000000, transcendentals=0
        ),
        name="assemble",
    )(field, side)


def sweep_kernel(odd_ref, *refs):
    rows_refs = refs[:4]
    coef_a_ref, step_a_ref, coef_b_ref, step_b_ref, wall_ref, out_ref, motion_ref, edge_ref = refs[4:]
    odd = odd_ref[0] == 1
    planes = motion_ref.shape[1]
    middle = planes // 2
    for c in range(3):
        fill_rows(motion_ref, rows_refs, odd, c, c)
    fill_rows(edge_ref, rows_refs, odd, 3, 0)
    lane = lax.broadcasted_iota(I32, (8, 128), 1)
    first, last = lane == 0, lane == 127

    def neighbours(k):
        side = edge_ref[0, k]
        near = {}
        for c in range(3):
            here = motion_ref[c, k]
            before = pltpu.roll(side, 128 - c, 1) if c else side
            beyond = pltpu.roll(side, 2 - c, 1) if c < 2 else side
            for x, value in (
                (-1, jnp.where(first, before, pltpu.roll(here, 1, 1))),
                (0, here),
                (1, jnp.where(last, beyond, pltpu.roll(here, 127, 1))),
            ):
                near[c, 0, x] = value
                near[c, -1, x] = pltpu.roll(value, 1, 0)
                near[c, 1, x] = pltpu.roll(value, 7, 0)
        return near

    def reach(force, near, plane, z):
        coef_ref, at = (coef_a_ref, plane) if plane < middle else (coef_b_ref, plane - middle + 1)
        for y in (-1, 0, 1):
            for x in (-1, 0, 1):
                m = SLOT_OF.get((x, y, z), SELF)
                block = [coef_ref[at, m, e] for e in range(6)]
                for p in range(3):
                    term = sum(block[ENTRY[p][q]] * near[q, y, x] for q in range(3))
                    force[p] = term if force[p] is None else force[p] + term

    for sweep in range(SWEEPS):
        low, high = sweep + 1, planes - 2 - sweep
        force = {k: [None] * 3 for k in range(low, high + 1)}
        for k in range(low - 1, high + 2):
            near = neighbours(k)
            for z in (1, 0, -1):
                if low <= k - z <= high:
                    reach(force[k - z], near, k - z, z)
            done = k - 1
            if done in force:
                step_ref, at = (step_a_ref, done) if done < middle else (step_b_ref, done - middle + 1)
                for p in range(3):
                    motion_ref[p, done] = motion_ref[p, done] - step_ref[at, p] * force[done][p]
    for c in range(3):
        for y in range(2):
            out_ref[c, y, :, :128] = wall_ref[c, y]
            out_ref[c, y, :, 128:] = motion_ref[c, DEPTH : planes - DEPTH, y, :]


def sweeps(odd, rows, lower, upper, wall):
    planes = rows[0].shape[2]
    return pl.pallas_call(
        sweep_kernel,
        out_shape=jax.ShapeDtypeStruct((3, 2, planes - 2 * DEPTH, 256), F32),
        in_specs=[SMEM] + [VMEM] * 9,
        out_specs=VMEM,
        scratch_shapes=[
            pltpu.VMEM((3, planes, 8, 128), F32),
            pltpu.VMEM((1, planes, 8, 128), F32),
        ],
        compiler_params=params(20),
        name="sweeps",
    )(odd, *rows, *lower, *upper, wall)


def swap(block, partner):
    struct_count, fluid_count = lax.axis_size("struct"), lax.axis_size("fluid")
    route = []
    for s in range(struct_count):
        for f in range(fluid_count):
            to_s, to_f = partner(s, f)
            route.append((s * fluid_count + f, to_s * fluid_count + to_f % fluid_count))
    return lax.ppermute(block, BOTH, route)


def planes_apart(parts):
    _, for_pair, for_next = parts
    return (
        swap(for_pair, lambda s, f: (s, f ^ 1)),
        swap(for_next, lambda s, f: (s, ((f - 1) ^ 1) + 1)),
    )


def widened(even, out_ref, to, whole, in_pair, next_pair):
    count = whole.shape[1]
    out_ref[to, :, :DEPTH] = jnp.where(even, next_pair, in_pair)
    out_ref[to, :, DEPTH : DEPTH + count] = whole
    out_ref[to, :, DEPTH + count :] = jnp.where(even, in_pair, next_pair)


def widen_fields_kernel(even_ref, whole_ref, pair_ref, next_ref, lattice_ref, prev_ref, plan_ref):
    even = even_ref[0] == 1
    for c in range(8):
        out_ref, to = (lattice_ref, c) if c < 5 else (prev_ref, c - 5)
        widened(even, out_ref, to, whole_ref[c], pair_ref[c], next_ref[c])
    plan_ref[...] = whole_ref[8:]


def widen_fields(even, whole, in_pair, next_pair):
    _, rows, count, lanes = whole.shape
    return pl.pallas_call(
        widen_fields_kernel,
        out_shape=(
            jax.ShapeDtypeStruct((5, rows, count + 2 * DEPTH, lanes), F32),
            jax.ShapeDtypeStruct((3, rows, count + 2 * DEPTH, lanes), F32),
            jax.ShapeDtypeStruct((8, rows, count, lanes), F32),
        ),
        in_specs=[SMEM] + [VMEM] * 3,
        out_specs=(VMEM,) * 3,
        compiler_params=params(4),
        name="widen_fields",
    )(even, whole, in_pair, next_pair)


def widen_wall_kernel(even_ref, prev_ref, columns_ref, pair_ref, next_ref, out_ref):
    out_ref[:3] = prev_ref[...]
    widened(even_ref[0] == 1, out_ref, 3, columns_ref[0], pair_ref[0], next_ref[0])


def widen_wall(even, prev, columns, in_pair, next_pair):
    return pl.pallas_call(
        widen_wall_kernel,
        out_shape=jax.ShapeDtypeStruct((4, *prev.shape[1:]), F32),
        in_specs=[SMEM] + [VMEM] * 4,
        out_specs=VMEM,
        compiler_params=params(4),
        name="widen_wall",
    )(even, prev, columns, in_pair, next_pair)


def all_rows(block):
    return [block] + [swap(block, lambda s, f, m=m: (s ^ m, f)) for m in (1, 2, 3)]


def shards(shell_motion, owner, stencil_slot, stencil_weight, prev_motion, node_offset, cell_split):
    odd = (lax.axis_index("struct") & 1).astype(I32).reshape(1)
    even = 1 - (lax.axis_index("fluid") & 1).astype(I32).reshape(1)
    packed = pack(owner, shell_motion)
    sent = fields(even, node_offset, cell_split, prev_motion, stencil_slot, stencil_weight)
    apart = planes_apart(sent)
    packed, apart = lax.optimization_barrier((packed, apart))
    lattice, prev, plan = widen_fields(even, sent[0], *apart)
    field, side = setup(odd, all_rows(lattice))
    received = lax.all_to_all(packed, BOTH, split_axis=0, concat_axis=0, tiled=True)
    received, field, side = lax.optimization_barrier((received, field, side))
    sent = wall_columns(even, received, plan)
    field, side, *sent = lax.optimization_barrier((field, side, *sent))
    apart = planes_apart(sent)
    lower = assemble(field, side, 0, 8)
    lower, apart = lax.optimization_barrier((lower, apart))
    joined = widen_wall(even, prev, sent[0], *apart)
    field, side, received, joined = lax.optimization_barrier((field, side, received, joined))
    rows = all_rows(joined)
    upper = assemble(field, side, 7, 15)
    wall = gather(received, plan)
    return sweeps(odd, rows, lower, upper, wall)


def solution(mesh):
    return jax.shard_map(
        shards,
        mesh=mesh,
        in_specs=(
            P(None, BOTH),
            P(BOTH, None),
            P(None, "struct", "fluid", None),
            P(None, "struct", "fluid", None),
            P(None, "struct", "fluid", None),
            P(None, "struct", "fluid", None),
            P("struct", "fluid", None),
        ),
        out_specs=P(None, "struct", "fluid", None),
        check_vma=False,
    )
```

```python
from functools import partial

import jax
import jax.numpy as jnp
from jax import lax
from jax.experimental import pallas as pl
from jax.experimental.pallas import tpu as pltpu
from jax.sharding import PartitionSpec as P

SWEEPS = 4
RELAX_FACTOR = 0.5
STEP_ORDERS = ((0, 1, 2), (0, 2, 1), (1, 0, 2), (1, 2, 0), (2, 0, 1), (2, 1, 0))
BITS = (0, 1)
CORNERS = tuple((a, b, c) for a in BITS for b in BITS for c in BITS)
STEPS = tuple(
    (x, y, z) for z in (-1, 0, 1) for y in (-1, 0, 1) for x in (-1, 0, 1) if (x, y, z) != (0, 0, 0)
)
SLOT_OF = {step: k for k, step in enumerate(STEPS)}
SELF = len(STEPS)
ENTRY = ((0, 3, 4), (3, 1, 5), (4, 5, 2))
BOTH = ("struct", "fluid")
DEPTH = SWEEPS
SETUP_FLOPS, PLANE_FLOPS = 20000000, 20000000
FULL = 63
F32, BF16, I32 = jnp.float32, jnp.bfloat16, jnp.int32
VMEM = pl.BlockSpec(memory_space=pltpu.VMEM)
SMEM = pl.BlockSpec(memory_space=pltpu.SMEM)
HBM = pl.BlockSpec(memory_space=pltpu.HBM)


def fetch(sources, targets, semaphores):
    copies = [
        pltpu.make_async_copy(source, target, semaphores.at[k])
        for k, (source, target) in enumerate(zip(sources, targets))
    ]
    for copy in copies:
        copy.start()
    for copy in copies:
        copy.wait()


def params(mebibytes):
    return pltpu.CompilerParams(vmem_limit_bytes=int(mebibytes * 2**20))


def pack_kernel(owner_hbm, value_hbm, out_ref, left_ref, right_ref, owner_ref, value_ref, semaphores):
    fetch((owner_hbm, value_hbm), (owner_ref, value_ref), semaphores)
    count = owner_ref.shape[1]
    width = 256
    rows = lax.broadcasted_iota(I32, (width, width + 128), 0)
    columns = lax.broadcasted_iota(I32, (width, width + 128), 1)
    earlier = jnp.where((rows < columns) | (columns >= width), 1.0, 0.0).astype(BF16)
    owners = lax.broadcasted_iota(I32, (128, width), 0)
    pairs = lax.broadcasted_iota(I32, (64, width), 0)
    places = lax.broadcasted_iota(I32, (256, width), 0)
    base = jnp.zeros((128, 128), F32)
    for k in range(count // width):
        part = pl.ds(k * width, width)
        own = owner_ref[:, part]
        hit = owners == own
        before = jnp.dot(
            jnp.where(hit, 1.0, 0.0).astype(BF16), earlier, preferred_element_type=F32
        )
        running = before[:, :width] + jnp.concatenate([base, base], axis=1)
        rank = jnp.sum(jnp.where(hit, running, 0.0), axis=0, keepdims=True).astype(I32)
        base = base + before[:, width:]
        right_ref[:, part] = jnp.where(places == (own & 1) * 128 + rank, 1.0, 0.0).astype(BF16)
        half = pairs == (own >> 1)
        for c in range(3):
            value = value_ref[c : c + 1, part]
            high = value.astype(BF16).astype(F32)
            low = value - high
            left_ref[c * 64 : c * 64 + 64, part] = jnp.where(half, high, 0.0).astype(BF16)
            left_ref[192 + c * 64 : 256 + c * 64, part] = jnp.where(half, low, 0.0).astype(BF16)
    product = lax.dot_general(
        left_ref[...], right_ref[...], (((1,), (1,)), ((), ())), preferred_element_type=F32
    )
    both = product[:192] + product[192:]
    for c in range(3):
        for h in range(2):
            out_ref[pl.ds(h, 64, stride=2), c, :] = both[c * 64 : c * 64 + 64, h * 128 : h * 128 + 128]


def pack(owner, shell_motion):
    count = shell_motion.shape[1]
    return pl.pallas_call(
        pack_kernel,
        out_shape=jax.ShapeDtypeStruct((128, 3, 128), F32),
        in_specs=[HBM] * 2,
        out_specs=VMEM,
        scratch_shapes=[
            pltpu.VMEM((384, count), BF16),
            pltpu.VMEM((256, count), BF16),
            pltpu.VMEM((1, count), I32),
            pltpu.VMEM((3, count), F32),
            pltpu.SemaphoreType.DMA((2,)),
        ],
        compiler_params=params(FULL),
        name="pack",
    )(owner.reshape(1, count), shell_motion)


def payload(kept, sent):
    return (
        jax.ShapeDtypeStruct((kept, 2, 8, 128), F32),
        jax.ShapeDtypeStruct((sent, 2, DEPTH, 128), F32),
        jax.ShapeDtypeStruct((sent, 2, DEPTH, 128), F32),
    )


def emit(refs, even, channel, y, value):
    whole_ref, pair_ref, next_ref = refs
    first, last = value[:DEPTH], value[DEPTH:]
    whole_ref[channel, y] = value
    pair_ref[channel, y] = jnp.where(even, last, first)
    next_ref[channel, y] = jnp.where(even, first, last)


def fields_kernel(even_ref, offset_hbm, split_hbm, prev_hbm, slot_hbm, weight_hbm, *refs):
    out_refs, (slot_ref, weight_ref, offset_ref, split_ref, prev_ref, semaphores) = refs[:3], refs[3:]
    fetch(
        (offset_hbm, split_hbm, prev_hbm, slot_hbm, weight_hbm),
        (offset_ref, split_ref, prev_ref, slot_ref, weight_ref),
        semaphores,
    )
    out_refs[0][8:12] = slot_ref[...].astype(F32)
    out_refs[0][12:16] = weight_ref[...]
    even = even_ref[0] == 1
    lane = lax.broadcasted_iota(I32, (8, 128), 1)
    for y in range(2):
        code = split_ref[y].astype(F32)
        columns = jnp.where(lane == 3, pltpu.roll(code[:, :128], 4, 1), 0.0)
        for p in range(3):
            wall, free = offset_ref[p, y, :, :128], offset_ref[p, y, :, 128:]
            columns = jnp.where(lane == p, pltpu.roll(wall, p + 1, 1), columns)
            columns = jnp.where(lane == 4 + p, pltpu.roll(free, 4 + p, 1), columns)
            columns = jnp.where(lane == 125 + p, pltpu.roll(wall, 125 + p, 1), columns)
            emit(out_refs, even, p, y, free)
            emit(out_refs, even, 5 + p, y, prev_ref[p, y, :, 128:])
        emit(out_refs, even, 3, y, code[:, 128:])
        emit(out_refs, even, 4, y, columns)


def fields(even, node_offset, cell_split, prev_motion, stencil_slot, stencil_weight):
    return pl.pallas_call(
        fields_kernel,
        out_shape=payload(16, 8),
        in_specs=[SMEM] + [HBM] * 5,
        out_specs=(VMEM,) * 3,
        scratch_shapes=[
            pltpu.VMEM(stencil_slot.shape, I32),
            pltpu.VMEM(stencil_weight.shape, F32),
            pltpu.VMEM(node_offset.shape, F32),
            pltpu.VMEM(cell_split.shape, I32),
            pltpu.VMEM(prev_motion.shape, F32),
            pltpu.SemaphoreType.DMA((5,)),
        ],
        compiler_params=params(FULL),
        name="fields",
    )(even, node_offset, cell_split, prev_motion, stencil_slot, stencil_weight)


def columns_kernel(even_ref, received_ref, plan_ref, *refs):
    column_refs, table_ref = refs[:3], refs[3]
    for c in range(3):
        flat = received_ref[:, c, :]
        high = flat.astype(BF16).astype(F32)
        low = flat - high
        for part, base in ((high, 0), (low, 192)):
            at = slice(base + c * 64, base + c * 64 + 64)
            table_ref[:128, at] = part[:, :64].astype(BF16)
            table_ref[128:, at] = part[:, 64:].astype(BF16)

    def stacked(first):
        return jnp.concatenate(
            [
                plan_ref[first + t, y, :, x : x + 1]
                for t in range(4)
                for y in range(2)
                for x in (127, 0)
            ]
        )

    slot = stacked(0).astype(I32)
    weight = stacked(4)
    pick = ((slot >> 6) & 1) * 128 + (slot >> 7)
    hot = jnp.where(lax.broadcasted_iota(I32, (128, 256), 1) == pick, 1.0, 0.0).astype(BF16)
    found = jnp.dot(hot, table_ref[...], preferred_element_type=F32)
    found = found[:, :192] + found[:, 192:]
    share = jnp.where(lax.broadcasted_iota(I32, (128, 192), 1) % 64 == (slot & 63), weight, 0.0) * found
    share = share[:32] + share[32:64] + share[64:96] + share[96:]
    values = [jnp.sum(share[:, c * 64 : c * 64 + 64], axis=1, keepdims=True) for c in range(3)]
    lane = lax.broadcasted_iota(I32, (8, 128), 1)
    for y in range(2):
        columns = jnp.zeros((8, 128), F32)
        for c in range(3):
            columns = jnp.where(lane == c, values[c][y * 16 : y * 16 + 8], columns)
            columns = jnp.where(lane == 125 + c, values[c][y * 16 + 8 : y * 16 + 16], columns)
        emit(column_refs, even_ref[0] == 1, 0, y, columns)


def wall_columns(even, received, plan):
    return pl.pallas_call(
        columns_kernel,
        out_shape=payload(1, 1),
        in_specs=[SMEM] + [VMEM] * 2,
        out_specs=(VMEM,) * 3,
        scratch_shapes=[pltpu.VMEM((256, 384), BF16)],
        compiler_params=params(8),
        name="columns",
    )(even, received, plan)


def gather_kernel(received_ref, plan_ref, out_ref, table_ref):
    for c in range(3):
        flat = received_ref[:, c, :].T
        high = flat.astype(BF16).astype(F32)
        low = flat - high
        for part, base in ((high, 0), (low, 192)):
            at = base + c * 64
            table_ref[at : at + 64, :128] = part[:64].astype(BF16)
            table_ref[at : at + 64, 128:] = part[64:].astype(BF16)
    table = table_ref[...]
    picks = lax.broadcasted_iota(I32, (256, 256), 0)
    places = lax.broadcasted_iota(I32, (64, 256), 0)
    for y in range(2):
        for z in range(0, 8, 2):
            total = [jnp.zeros((64, 256), F32) for _ in range(3)]
            for t in range(4):
                slot, weight = [
                    jnp.concatenate([plan_ref[first + t, y, z + k : z + k + 1, :] for k in BITS], axis=1)
                    for first in (0, 4)
                ]
                slot = slot.astype(I32)
                pick = ((slot >> 6) & 1) * 128 + (slot >> 7)
                hot = jnp.where(picks == pick, 1.0, 0.0).astype(BF16)
                found = jnp.dot(table, hot, preferred_element_type=F32)
                share = jnp.where(places == (slot & 63), weight, 0.0)
                for c in range(3):
                    at = c * 64
                    total[c] = total[c] + share * (found[at : at + 64] + found[at + 192 : at + 256])
            for c in range(3):
                line = jnp.sum(total[c], axis=0, keepdims=True)
                for k in BITS:
                    out_ref[c, y, z + k : z + k + 1, :] = line[:, k * 128 : k * 128 + 128]


def gather(received, plan):
    return pl.pallas_call(
        gather_kernel,
        out_shape=jax.ShapeDtypeStruct((3, 2, 8, 128), F32),
        in_specs=[VMEM] * 2,
        out_specs=VMEM,
        scratch_shapes=[pltpu.VMEM((384, 256), BF16)],
        compiler_params=params(8),
        cost_estimate=pl.CostEstimate(flops=60000000, bytes_accessed=1000000, transcendentals=0),
        name="gather",
    )(received, plan)


def back_y(values):
    return [pltpu.roll(v, 1, 0) for v in values]


def plus(u, v):
    return [p + q for p, q in zip(u, v)]


def cross(u, v):
    return [
        u[1] * v[2] - u[2] * v[1],
        u[2] * v[0] - u[0] * v[2],
        u[0] * v[1] - u[1] * v[0],
    ]


def cell_blocks(corner, code):
    flip_y = code >= 2
    flip_z = (code == 1) | (code == 3)
    sign_y = jnp.where(flip_y, -1.0, 1.0)
    sign_z = jnp.where(flip_z, -1.0, 1.0)
    named = {}
    for a, b, c in CORNERS:
        named[a, b, c] = [jnp.where(flip_y, corner[a, 1 - b, c][p], corner[a, b, c][p]) for p in range(3)]
    named = {
        (a, b, c): [jnp.where(flip_z, named[a, b, 1 - c][p], named[a, b, c][p]) for p in range(3)]
        for a, b, c in CORNERS
    }
    edge = {}
    for v in CORNERS[1:]:
        moved = [named[v][p] - named[0, 0, 0][p] for p in range(3)]
        if v[0]:
            moved[0] = moved[0] + 1.0
        if v[1]:
            moved[1] = moved[1] + sign_y
        if v[2]:
            moved[2] = moved[2] + sign_z
        edge[v] = moved
    top = (1, 1, 1)
    over = {v: cross(edge[v], edge[top]) for v in CORNERS[1:-1]}
    blocks = {}
    for order in STEP_ORDERS:
        at = [0, 0, 0]
        path = [(0, 0, 0)]
        for axis in order:
            at[axis] = 1
            path.append(tuple(at))
        one, two = path[1], path[2]
        third = cross(edge[one], edge[two])
        volume = sum(edge[one][p] * over[two][p] for p in range(3))
        inverse = 1.0 / volume
        minus = -inverse
        grad = [None, [w * inverse for w in over[two]], [w * minus for w in over[one]], [w * inverse for w in third]]
        grad[0] = [grad[1][p] + grad[2][p] + grad[3][p] for p in range(3)]
        for i in range(4):
            for j in range(i + 1, 4):
                g, h = grad[i], grad[j]
                block = [g[p] * h[p] for p in range(3)]
                block += [g[p] * h[q] + g[q] * h[p] for p, q in ((0, 1), (0, 2), (1, 2))]
                key = (path[i], path[j])
                blocks[key] = plus(blocks[key], block) if key in blocks else block
    for (v, _), block in blocks.items():
        trace = block[0] + block[1] + block[2]
        block[:3] = [same + same + trace for same in block[:3]]
        if v == (0, 0, 0):
            block[:] = [-w for w in block]

    def pick(mask, yes, no):
        return [jnp.where(mask, y, n) for y, n in zip(yes, no)]

    def keep(mask, values):
        return [jnp.where(mask, v, 0.0) for v in values]

    along_x = {(b, c): blocks[(0, b, c), (1, b, c)] for b in BITS for c in BITS}
    along_x = {(b, c): pick(flip_y, along_x[1 - b, c], along_x[b, c]) for b, c in along_x}
    along_x = {(b, c): pick(flip_z, along_x[b, 1 - c], along_x[b, c]) for b, c in along_x}
    along_y = {(a, c): blocks[(a, 0, c), (a, 1, c)] for a in BITS for c in BITS}
    along_y = {(a, c): pick(flip_z, along_y[a, 1 - c], along_y[a, c]) for a, c in along_y}
    along_z = {(a, b): blocks[(a, b, 0), (a, b, 1)] for a in BITS for b in BITS}
    along_z = {(a, b): pick(flip_y, along_z[a, 1 - b], along_z[a, b]) for a, b in along_z}
    no_y, no_z, unlike = ~flip_y, ~flip_z, flip_y ^ flip_z
    in_xy = [blocks[(0, 0, c), (1, 1, c)] for c in BITS]
    in_xy = [pick(flip_z, in_xy[1 - c], in_xy[c]) for c in BITS]
    in_xz = [blocks[(0, b, 0), (1, b, 1)] for b in BITS]
    in_xz = [pick(flip_y, in_xz[1 - b], in_xz[b]) for b in BITS]
    in_yz = [blocks[(a, 0, 0), (a, 1, 1)] for a in BITS]
    body = blocks[(0, 0, 0), top]
    return dict(
        x=along_x,
        y=along_y,
        z=along_z,
        xy=[(keep(no_y, v), keep(flip_y, v)) for v in in_xy],
        xz=[(keep(no_z, v), keep(flip_z, v)) for v in in_xz],
        yz=[(keep(~unlike, v), keep(unlike, v)) for v in in_yz],
        xyz={
            (0, 0): keep(no_y & no_z, body),
            (0, 1): keep(no_y & flip_z, body),
            (1, 0): keep(flip_y & no_z, body),
            (1, 1): keep(flip_y & flip_z, body),
        },
    )


def fill_rows(target_ref, rows_refs, odd, channel, to):
    own, swap1, swap2, swap3 = rows_refs
    for r in range(2):
        one, three = swap1[channel, r], swap3[channel, r]
        for place, value in (
            (0, own[channel, r]),
            (2, jnp.where(odd, three, one)),
            (4, swap2[channel, r]),
            (6, jnp.where(odd, one, three)),
        ):
            target_ref[to, :, place + r, :] = value


MOVING = ("z", "xz_up", "xz_down", "yz_up", "yz_down", "b00", "b01", "b10", "b11") + tuple(
    (name, c) for c in BITS for name in ("x", "y", "up", "down")
)


def node_parts(kinds):
    x, y, z = kinds["x"], kinds["y"], kinds["z"]
    (xz_up0, xz_down0), (xz_up1, xz_down1) = kinds["xz"]
    (yz_up0, yz_down0), (yz_up1, yz_down1) = kinds["yz"]
    body = {key: (v, back_y(v)) for key, v in kinds["xyz"].items()}
    moving = {
        "z": plus(z[1, 0], back_y(z[1, 1])),
        "xz_up": plus(xz_up0, back_y(xz_up1)),
        "xz_down": plus(xz_down0, back_y(xz_down1)),
        "yz_up": yz_up1,
        "yz_down": yz_down1,
        "b00": body[0, 0][1],
        "b01": body[0, 1][1],
        "b10": body[1, 0][0],
        "b11": body[1, 1][0],
    }
    still = {
        "z": plus(z[0, 0], back_y(z[0, 1])),
        "yz_up": yz_up0,
        "yz_down": yz_down0,
        "b00": body[0, 0][0],
        "b01": body[0, 1][0],
        "b10": body[1, 0][1],
        "b11": body[1, 1][1],
    }
    for c in BITS:
        up, down = kinds["xy"][c]
        moving["x", c] = plus(x[0, c], back_y(x[1, c]))
        moving["y", c] = y[1, c]
        moving["up", c] = back_y(up)
        moving["down", c] = down
        still["y", c] = y[0, c]
        still["up", c] = up
        still["down", c] = back_y(down)
    return moving, still


def setup_kernel(odd_ref, own_ref, swap1_ref, swap2_ref, swap3_ref, _, field_ref, side_ref):
    odd = odd_ref[0] == 1
    for c in range(5):
        fill_rows(field_ref, (own_ref, swap1_ref, swap2_ref, swap3_ref), odd, c, c)
    planes = field_ref.shape[1]
    gap = 128 // planes
    lane = lax.broadcasted_iota(I32, (8, 128), 1)

    packed = jnp.zeros((8, 128), F32)
    for k in range(planes):
        packed = jnp.where(lane // gap == k, pltpu.roll(field_ref[4, k], k * gap, 1), packed)
    corner = {}
    for a in BITS:
        for p in range(3):
            low = pltpu.roll(packed, 128 - (4 * a + p), 1) if a or p else packed
            for c, plane in ((0, low), (1, pltpu.roll(low, 128 - gap, 1))):
                corner.setdefault((a, 0, c), []).append(plane)
                corner.setdefault((a, 1, c), []).append(pltpu.roll(plane, 7, 0))
    moving, _ = node_parts(cell_blocks(corner, pltpu.roll(packed, 125, 1)))
    for m, name in enumerate(MOVING):
        for e in range(6):
            side_ref[m, e] = moving[name][e]


def setup(odd, rows, after):
    planes = rows[0].shape[2]
    return pl.pallas_call(
        setup_kernel,
        out_shape=(
            jax.ShapeDtypeStruct((5, planes, 8, 128), F32),
            jax.ShapeDtypeStruct((len(MOVING), 6, 8, 128), F32),
        ),
        in_specs=[SMEM] + [VMEM] * 5,
        out_specs=(VMEM,) * 2,
        compiler_params=params(4),
        cost_estimate=pl.CostEstimate(flops=SETUP_FLOPS, bytes_accessed=1000000, transcendentals=0),
        name="setup",
    )(odd, *rows, after)


def assemble_kernel(start, stop, field_ref, side_ref, coef_ref, step_ref):
    planes = field_ref.shape[1]
    gap = 128 // planes
    lane = lax.broadcasted_iota(I32, (8, 128), 1)
    first, last = lane == 0, lane == 127

    def cells(k, _):
        corner = {}
        for c in BITS:
            edge = field_ref[4, k + c]
            edges = (edge, pltpu.roll(edge, 7, 0))
            for p in range(3):
                low = field_ref[p, k + c]
                for b, row in ((0, low), (1, pltpu.roll(low, 7, 0))):
                    beyond = pltpu.roll(edges[b], 2 - p, 1) if p < 2 else edges[b]
                    corner.setdefault((0, b, c), []).append(row)
                    corner.setdefault((1, b, c), []).append(jnp.where(last, beyond, pltpu.roll(row, 127, 1)))
        moving, still = node_parts(cell_blocks(corner, field_ref[3, k]))
        shift = 128 - k * gap

        def back_x(name):
            m = MOVING.index(name)
            return [
                jnp.where(first, pltpu.roll(side_ref[m, e], shift, 1), pltpu.roll(moving[name][e], 1, 1))
                for e in range(6)
            ]

        def put(plane, step, values):
            for e in range(6):
                coef_ref[plane, SLOT_OF[step], e] = values[e]

        def add(plane, step, values):
            at = SLOT_OF[step]
            for e in range(6):
                coef_ref[plane, at, e] = coef_ref[plane, at, e] + values[e]

        low, high = k - start, k + 1 - start
        s = plus(still["z"], back_x("z"))
        put(low, (0, 0, 1), s)
        put(high, (0, 0, -1), s)
        put(low, (1, 0, 1), moving["xz_up"])
        put(high, (-1, 0, -1), back_x("xz_up"))
        put(high, (1, 0, -1), moving["xz_down"])
        put(low, (-1, 0, 1), back_x("xz_down"))
        s = plus(still["yz_up"], back_x("yz_up"))
        put(low, (0, 1, 1), s)
        put(high, (0, -1, -1), back_y(s))
        s = plus(still["yz_down"], back_x("yz_down"))
        put(high, (0, 1, -1), s)
        put(low, (0, -1, 1), back_y(s))
        put(low, (1, 1, 1), still["b00"])
        put(high, (-1, -1, -1), back_x("b00"))
        put(high, (1, 1, -1), still["b01"])
        put(low, (-1, -1, 1), back_x("b01"))
        put(low, (1, -1, 1), still["b10"])
        put(high, (-1, 1, -1), back_x("b10"))
        put(high, (1, -1, -1), still["b11"])
        put(low, (-1, 1, 1), back_x("b11"))
        for c, plane, store in ((0, low, add), (1, high, put)):
            store(plane, (1, 0, 0), moving["x", c])
            store(plane, (-1, 0, 0), back_x(("x", c)))
            s = plus(still["y", c], back_x(("y", c)))
            store(plane, (0, 1, 0), s)
            store(plane, (0, -1, 0), back_y(s))
            store(plane, (1, 1, 0), still["up", c])
            store(plane, (-1, -1, 0), back_x(("up", c)))
            store(plane, (1, -1, 0), still["down", c])
            store(plane, (-1, 1, 0), back_x(("down", c)))
        return 0

    lax.fori_loop(start, stop, cells, 0, unroll=8)

    def selves(k, _):
        for e in range(6):
            total = coef_ref[k, 0, e]
            for m in range(1, SELF):
                total = total + coef_ref[k, m, e]
            coef_ref[k, SELF, e] = -total
            if e < 3:
                step_ref[k, e] = -RELAX_FACTOR / total
        return 0

    lax.fori_loop(1, stop - start, selves, 0, unroll=7)


def assemble(field, side, start, stop):
    return pl.pallas_call(
        partial(assemble_kernel, start, stop),
        out_shape=(
            jax.ShapeDtypeStruct((stop - start + 1, SELF + 1, 6, 8, 128), F32),
            jax.ShapeDtypeStruct((stop - start + 1, 3, 8, 128), F32),
        ),
        in_specs=[VMEM] * 2,
        out_specs=(VMEM,) * 2,
        compiler_params=params(12),
        cost_estimate=pl.CostEstimate(
            flops=PLANE_FLOPS * (stop - start), bytes_accessed=1000000, transcendentals=0
        ),
        name="assemble",
    )(field, side)


def sweep_kernel(odd_ref, *refs):
    rows_refs = refs[:4]
    coef_a_ref, step_a_ref, coef_b_ref, step_b_ref, wall_ref, out_ref, motion_ref, edge_ref = refs[4:]
    odd = odd_ref[0] == 1
    planes = motion_ref.shape[1]
    middle = planes // 2
    for c in range(3):
        fill_rows(motion_ref, rows_refs, odd, c, c)
    fill_rows(edge_ref, rows_refs, odd, 3, 0)
    lane = lax.broadcasted_iota(I32, (8, 128), 1)
    first, last = lane == 0, lane == 127

    def neighbours(k):
        side = edge_ref[0, k]
        near = {}
        for c in range(3):
            here = motion_ref[c, k]
            before = pltpu.roll(side, 128 - c, 1) if c else side
            beyond = pltpu.roll(side, 2 - c, 1) if c < 2 else side
            for x, value in (
                (-1, jnp.where(first, before, pltpu.roll(here, 1, 1))),
                (0, here),
                (1, jnp.where(last, beyond, pltpu.roll(here, 127, 1))),
            ):
                near[c, 0, x] = value
                near[c, -1, x] = pltpu.roll(value, 1, 0)
                near[c, 1, x] = pltpu.roll(value, 7, 0)
        return near

    def reach(force, near, plane, z):
        coef_ref, at = (coef_a_ref, plane) if plane < middle else (coef_b_ref, plane - middle + 1)
        for y in (-1, 0, 1):
            for x in (-1, 0, 1):
                m = SLOT_OF.get((x, y, z), SELF)
                block = [coef_ref[at, m, e] for e in range(6)]
                for p in range(3):
                    term = sum(block[ENTRY[p][q]] * near[q, y, x] for q in range(3))
                    force[p] = term if force[p] is None else force[p] + term

    for sweep in range(SWEEPS):
        low, high = sweep + 1, planes - 2 - sweep
        force = {k: [None] * 3 for k in range(low, high + 1)}
        for k in range(low - 1, high + 2):
            near = neighbours(k)
            for z in (1, 0, -1):
                if low <= k - z <= high:
                    reach(force[k - z], near, k - z, z)
            done = k - 1
            if done in force:
                step_ref, at = (step_a_ref, done) if done < middle else (step_b_ref, done - middle + 1)
                for p in range(3):
                    motion_ref[p, done] = motion_ref[p, done] - step_ref[at, p] * force[done][p]
    for c in range(3):
        for y in range(2):
            out_ref[c, y, :, :128] = wall_ref[c, y]
            out_ref[c, y, :, 128:] = motion_ref[c, DEPTH : planes - DEPTH, y, :]


def sweeps(odd, rows, lower, upper, wall):
    planes = rows[0].shape[2]
    return pl.pallas_call(
        sweep_kernel,
        out_shape=jax.ShapeDtypeStruct((3, 2, planes - 2 * DEPTH, 256), F32),
        in_specs=[SMEM] + [VMEM] * 9,
        out_specs=VMEM,
        scratch_shapes=[
            pltpu.VMEM((3, planes, 8, 128), F32),
            pltpu.VMEM((1, planes, 8, 128), F32),
        ],
        compiler_params=params(20),
        name="sweeps",
    )(odd, *rows, *lower, *upper, wall)


def swap(block, partner):
    struct_count, fluid_count = lax.axis_size("struct"), lax.axis_size("fluid")
    route = []
    for s in range(struct_count):
        for f in range(fluid_count):
            to_s, to_f = partner(s, f)
            route.append((s * fluid_count + f, to_s * fluid_count + to_f % fluid_count))
    return lax.ppermute(block, BOTH, route)


def planes_apart(parts):
    _, for_pair, for_next = parts
    return (
        swap(for_pair, lambda s, f: (s, f ^ 1)),
        swap(for_next, lambda s, f: (s, ((f - 1) ^ 1) + 1)),
    )


def widened(even, out_ref, to, whole, in_pair, next_pair):
    count = whole.shape[1]
    out_ref[to, :, :DEPTH] = jnp.where(even, next_pair, in_pair)
    out_ref[to, :, DEPTH : DEPTH + count] = whole
    out_ref[to, :, DEPTH + count :] = jnp.where(even, in_pair, next_pair)


def widen_fields_kernel(even_ref, whole_ref, pair_ref, next_ref, lattice_ref, prev_ref, plan_ref):
    even = even_ref[0] == 1
    for c in range(8):
        out_ref, to = (lattice_ref, c) if c < 5 else (prev_ref, c - 5)
        widened(even, out_ref, to, whole_ref[c], pair_ref[c], next_ref[c])
    plan_ref[...] = whole_ref[8:]


def widen_fields(even, whole, in_pair, next_pair):
    _, rows, count, lanes = whole.shape
    return pl.pallas_call(
        widen_fields_kernel,
        out_shape=(
            jax.ShapeDtypeStruct((5, rows, count + 2 * DEPTH, lanes), F32),
            jax.ShapeDtypeStruct((3, rows, count + 2 * DEPTH, lanes), F32),
            jax.ShapeDtypeStruct((8, rows, count, lanes), F32),
        ),
        in_specs=[SMEM] + [VMEM] * 3,
        out_specs=(VMEM,) * 3,
        compiler_params=params(4),
        name="widen_fields",
    )(even, whole, in_pair, next_pair)


def widen_wall_kernel(even_ref, prev_ref, columns_ref, pair_ref, next_ref, out_ref):
    out_ref[:3] = prev_ref[...]
    widened(even_ref[0] == 1, out_ref, 3, columns_ref[0], pair_ref[0], next_ref[0])


def widen_wall(even, prev, columns, in_pair, next_pair):
    return pl.pallas_call(
        widen_wall_kernel,
        out_shape=jax.ShapeDtypeStruct((4, *prev.shape[1:]), F32),
        in_specs=[SMEM] + [VMEM] * 4,
        out_specs=VMEM,
        compiler_params=params(4),
        name="widen_wall",
    )(even, prev, columns, in_pair, next_pair)


def all_rows(block):
    return [block] + [swap(block, lambda s, f, m=m: (s ^ m, f)) for m in (1, 2, 3)]


def shards(shell_motion, owner, stencil_slot, stencil_weight, prev_motion, node_offset, cell_split):
    odd = (lax.axis_index("struct") & 1).astype(I32).reshape(1)
    even = 1 - (lax.axis_index("fluid") & 1).astype(I32).reshape(1)
    packed = pack(owner, shell_motion)
    sent = fields(even, node_offset, cell_split, prev_motion, stencil_slot, stencil_weight)
    apart = planes_apart(sent)
    packed, apart = lax.optimization_barrier((packed, apart))
    lattice, prev, plan = widen_fields(even, sent[0], *apart)
    rows = all_rows(lattice)
    received = lax.all_to_all(packed, BOTH, split_axis=0, concat_axis=0, tiled=True)
    sent = wall_columns(even, received, plan)
    field, side = setup(odd, rows, sent[0])
    apart = planes_apart(sent)
    lower = assemble(field, side, 0, 8)
    lower, apart = lax.optimization_barrier((lower, apart))
    joined = widen_wall(even, prev, sent[0], *apart)
    field, side, received, joined = lax.optimization_barrier((field, side, received, joined))
    rows = all_rows(joined)
    upper = assemble(field, side, 7, 15)
    wall = gather(received, plan)
    return sweeps(odd, rows, lower, upper, wall)


def solution(mesh):
    return jax.shard_map(
        shards,
        mesh=mesh,
        in_specs=(
            P(None, BOTH),
            P(BOTH, None),
            P(None, "struct", "fluid", None),
            P(None, "struct", "fluid", None),
            P(None, "struct", "fluid", None),
            P(None, "struct", "fluid", None),
            P("struct", "fluid", None),
        ),
        out_specs=P(None, "struct", "fluid", None),
        check_vma=False,
    )
```

```python
from functools import partial

import jax
import jax.numpy as jnp
from jax import lax
from jax.experimental import pallas as pl
from jax.experimental.pallas import tpu as pltpu
from jax.sharding import PartitionSpec as P

SWEEPS = 4
RELAX_FACTOR = 0.5
STEP_ORDERS = ((0, 1, 2), (0, 2, 1), (1, 0, 2), (1, 2, 0), (2, 0, 1), (2, 1, 0))
BITS = (0, 1)
CORNERS = tuple((a, b, c) for a in BITS for b in BITS for c in BITS)
STEPS = tuple(
    (x, y, z) for z in (-1, 0, 1) for y in (-1, 0, 1) for x in (-1, 0, 1) if (x, y, z) != (0, 0, 0)
)
SLOT_OF = {step: k for k, step in enumerate(STEPS)}
SELF = len(STEPS)
ENTRY = ((0, 3, 4), (3, 1, 5), (4, 5, 2))
BOTH = ("struct", "fluid")
DEPTH = SWEEPS
SETUP_FLOPS, PLANE_FLOPS = 20000000, 20000000
FULL = 63
F32, BF16, I32 = jnp.float32, jnp.bfloat16, jnp.int32
VMEM = pl.BlockSpec(memory_space=pltpu.VMEM)
SMEM = pl.BlockSpec(memory_space=pltpu.SMEM)
HBM = pl.BlockSpec(memory_space=pltpu.HBM)


def fetch(sources, targets, semaphores):
    copies = [
        pltpu.make_async_copy(source, target, semaphores.at[k])
        for k, (source, target) in enumerate(zip(sources, targets))
    ]
    for copy in copies:
        copy.start()
    for copy in copies:
        copy.wait()


def params(mebibytes):
    return pltpu.CompilerParams(vmem_limit_bytes=int(mebibytes * 2**20))


def pack(owner_ref, value_ref, out_ref, left_ref, right_ref):
    count = owner_ref.shape[1]
    width = 256
    rows = lax.broadcasted_iota(I32, (width, width + 128), 0)
    columns = lax.broadcasted_iota(I32, (width, width + 128), 1)
    earlier = jnp.where((rows < columns) | (columns >= width), 1.0, 0.0).astype(BF16)
    owners = lax.broadcasted_iota(I32, (128, width), 0)
    pairs = lax.broadcasted_iota(I32, (64, width), 0)
    places = lax.broadcasted_iota(I32, (256, width), 0)
    base = jnp.zeros((128, 128), F32)
    for k in range(count // width):
        part = pl.ds(k * width, width)
        own = owner_ref[:, part]
        hit = owners == own
        before = jnp.dot(
            jnp.where(hit, 1.0, 0.0).astype(BF16), earlier, preferred_element_type=F32
        )
        running = before[:, :width] + jnp.concatenate([base, base], axis=1)
        rank = jnp.sum(jnp.where(hit, running, 0.0), axis=0, keepdims=True).astype(I32)
        base = base + before[:, width:]
        right_ref[:, part] = jnp.where(places == (own & 1) * 128 + rank, 1.0, 0.0).astype(BF16)
        half = pairs == (own >> 1)
        for c in range(3):
            value = value_ref[c : c + 1, part]
            high = value.astype(BF16).astype(F32)
            low = value - high
            left_ref[c * 64 : c * 64 + 64, part] = jnp.where(half, high, 0.0).astype(BF16)
            left_ref[192 + c * 64 : 256 + c * 64, part] = jnp.where(half, low, 0.0).astype(BF16)
    product = lax.dot_general(
        left_ref[...], right_ref[...], (((1,), (1,)), ((), ())), preferred_element_type=F32
    )
    both = product[:192] + product[192:]
    for c in range(3):
        for h in range(2):
            out_ref[pl.ds(h, 64, stride=2), c, :] = both[c * 64 : c * 64 + 64, h * 128 : h * 128 + 128]


def payload(kept, sent):
    return (
        jax.ShapeDtypeStruct((kept, 2, 8, 128), F32),
        jax.ShapeDtypeStruct((sent, 2, DEPTH, 128), F32),
        jax.ShapeDtypeStruct((sent, 2, DEPTH, 128), F32),
    )


def emit(refs, even, channel, y, value):
    whole_ref, pair_ref, next_ref = refs
    first, last = value[:DEPTH], value[DEPTH:]
    whole_ref[channel, y] = value
    pair_ref[channel, y] = jnp.where(even, last, first)
    next_ref[channel, y] = jnp.where(even, first, last)


def fields(even, offset_ref, split_ref, prev_ref, slot_ref, weight_ref, out_refs):
    out_refs[0][8:12] = slot_ref[...].astype(F32)
    out_refs[0][12:16] = weight_ref[...]
    lane = lax.broadcasted_iota(I32, (8, 128), 1)
    for y in range(2):
        code = split_ref[y].astype(F32)
        columns = jnp.where(lane == 3, pltpu.roll(code[:, :128], 4, 1), 0.0)
        for p in range(3):
            wall, free = offset_ref[p, y, :, :128], offset_ref[p, y, :, 128:]
            columns = jnp.where(lane == p, pltpu.roll(wall, p + 1, 1), columns)
            columns = jnp.where(lane == 4 + p, pltpu.roll(free, 4 + p, 1), columns)
            columns = jnp.where(lane == 125 + p, pltpu.roll(wall, 125 + p, 1), columns)
            emit(out_refs, even, p, y, free)
            emit(out_refs, even, 5 + p, y, prev_ref[p, y, :, 128:])
        emit(out_refs, even, 3, y, code[:, 128:])
        emit(out_refs, even, 4, y, columns)


def first_kernel(even_ref, *refs):
    sources, outs, inputs = refs[:7], refs[7:11], refs[11:18]
    left_ref, right_ref, semaphores = refs[18:]
    fetch(sources, inputs, semaphores)
    fields(even_ref[0] == 1, *inputs[2:], outs[1:])
    pack(*inputs[:2], outs[0], left_ref, right_ref)


def pack_and_fields(even, owner, *others):
    count = owner.shape[0]
    inputs = (owner.reshape(1, count), *others)
    return pl.pallas_call(
        first_kernel,
        out_shape=(jax.ShapeDtypeStruct((128, 3, 128), F32), *payload(16, 8)),
        in_specs=[SMEM] + [HBM] * 7,
        out_specs=(VMEM,) * 4,
        scratch_shapes=[
            *(pltpu.VMEM(x.shape, x.dtype) for x in inputs),
            pltpu.VMEM((384, count), BF16),
            pltpu.VMEM((256, count), BF16),
            pltpu.SemaphoreType.DMA((7,)),
        ],
        compiler_params=params(FULL),
        name="first",
    )(even, *inputs)


def columns_kernel(even_ref, received_ref, plan_ref, *refs):
    column_refs, table_ref = refs[:3], refs[3]
    for c in range(3):
        flat = received_ref[:, c, :]
        high = flat.astype(BF16).astype(F32)
        low = flat - high
        for part, base in ((high, 0), (low, 192)):
            at = slice(base + c * 64, base + c * 64 + 64)
            table_ref[:128, at] = part[:, :64].astype(BF16)
            table_ref[128:, at] = part[:, 64:].astype(BF16)

    def stacked(first):
        return jnp.concatenate(
            [
                plan_ref[first + t, y, :, x : x + 1]
                for t in range(4)
                for y in range(2)
                for x in (127, 0)
            ]
        )

    slot = stacked(0).astype(I32)
    weight = stacked(4)
    pick = ((slot >> 6) & 1) * 128 + (slot >> 7)
    hot = jnp.where(lax.broadcasted_iota(I32, (128, 256), 1) == pick, 1.0, 0.0).astype(BF16)
    found = jnp.dot(hot, table_ref[...], preferred_element_type=F32)
    found = found[:, :192] + found[:, 192:]
    share = jnp.where(lax.broadcasted_iota(I32, (128, 192), 1) % 64 == (slot & 63), weight, 0.0) * found
    share = share[:32] + share[32:64] + share[64:96] + share[96:]
    values = [jnp.sum(share[:, c * 64 : c * 64 + 64], axis=1, keepdims=True) for c in range(3)]
    lane = lax.broadcasted_iota(I32, (8, 128), 1)
    for y in range(2):
        columns = jnp.zeros((8, 128), F32)
        for c in range(3):
            columns = jnp.where(lane == c, values[c][y * 16 : y * 16 + 8], columns)
            columns = jnp.where(lane == 125 + c, values[c][y * 16 + 8 : y * 16 + 16], columns)
        emit(column_refs, even_ref[0] == 1, 0, y, columns)


def wall_columns(even, received, plan):
    return pl.pallas_call(
        columns_kernel,
        out_shape=payload(1, 1),
        in_specs=[SMEM] + [VMEM] * 2,
        out_specs=(VMEM,) * 3,
        scratch_shapes=[pltpu.VMEM((256, 384), BF16)],
        compiler_params=params(8),
        name="columns",
    )(even, received, plan)


def gather_kernel(received_ref, plan_ref, out_ref, table_ref):
    for c in range(3):
        flat = received_ref[:, c, :].T
        high = flat.astype(BF16).astype(F32)
        low = flat - high
        for part, base in ((high, 0), (low, 192)):
            at = base + c * 64
            table_ref[at : at + 64, :128] = part[:64].astype(BF16)
            table_ref[at : at + 64, 128:] = part[64:].astype(BF16)
    table = table_ref[...]
    picks = lax.broadcasted_iota(I32, (256, 256), 0)
    places = lax.broadcasted_iota(I32, (64, 256), 0)
    for y in range(2):
        for z in range(0, 8, 2):
            total = [jnp.zeros((64, 256), F32) for _ in range(3)]
            for t in range(4):
                slot, weight = [
                    jnp.concatenate([plan_ref[first + t, y, z + k : z + k + 1, :] for k in BITS], axis=1)
                    for first in (0, 4)
                ]
                slot = slot.astype(I32)
                pick = ((slot >> 6) & 1) * 128 + (slot >> 7)
                hot = jnp.where(picks == pick, 1.0, 0.0).astype(BF16)
                found = jnp.dot(table, hot, preferred_element_type=F32)
                share = jnp.where(places == (slot & 63), weight, 0.0)
                for c in range(3):
                    at = c * 64
                    total[c] = total[c] + share * (found[at : at + 64] + found[at + 192 : at + 256])
            for c in range(3):
                line = jnp.sum(total[c], axis=0, keepdims=True)
                for k in BITS:
                    out_ref[c, y, z + k : z + k + 1, :] = line[:, k * 128 : k * 128 + 128]


def gather(received, plan):
    return pl.pallas_call(
        gather_kernel,
        out_shape=jax.ShapeDtypeStruct((3, 2, 8, 128), F32),
        in_specs=[VMEM] * 2,
        out_specs=VMEM,
        scratch_shapes=[pltpu.VMEM((384, 256), BF16)],
        compiler_params=params(8),
        cost_estimate=pl.CostEstimate(flops=60000000, bytes_accessed=1000000, transcendentals=0),
        name="gather",
    )(received, plan)


def back_y(values):
    return [pltpu.roll(v, 1, 0) for v in values]


def plus(u, v):
    return [p + q for p, q in zip(u, v)]


def cross(u, v):
    return [
        u[1] * v[2] - u[2] * v[1],
        u[2] * v[0] - u[0] * v[2],
        u[0] * v[1] - u[1] * v[0],
    ]


def cell_blocks(corner, code):
    flip_y = code >= 2
    flip_z = (code == 1) | (code == 3)
    sign_y = jnp.where(flip_y, -1.0, 1.0)
    sign_z = jnp.where(flip_z, -1.0, 1.0)
    named = {}
    for a, b, c in CORNERS:
        named[a, b, c] = [jnp.where(flip_y, corner[a, 1 - b, c][p], corner[a, b, c][p]) for p in range(3)]
    named = {
        (a, b, c): [jnp.where(flip_z, named[a, b, 1 - c][p], named[a, b, c][p]) for p in range(3)]
        for a, b, c in CORNERS
    }
    edge = {}
    for v in CORNERS[1:]:
        moved = [named[v][p] - named[0, 0, 0][p] for p in range(3)]
        if v[0]:
            moved[0] = moved[0] + 1.0
        if v[1]:
            moved[1] = moved[1] + sign_y
        if v[2]:
            moved[2] = moved[2] + sign_z
        edge[v] = moved
    top = (1, 1, 1)
    over = {v: cross(edge[v], edge[top]) for v in CORNERS[1:-1]}
    blocks = {}
    for order in STEP_ORDERS:
        at = [0, 0, 0]
        path = [(0, 0, 0)]
        for axis in order:
            at[axis] = 1
            path.append(tuple(at))
        one, two = path[1], path[2]
        third = cross(edge[one], edge[two])
        volume = sum(edge[one][p] * over[two][p] for p in range(3))
        inverse = 1.0 / volume
        minus = -inverse
        grad = [None, [w * inverse for w in over[two]], [w * minus for w in over[one]], [w * inverse for w in third]]
        grad[0] = [grad[1][p] + grad[2][p] + grad[3][p] for p in range(3)]
        for i in range(4):
            for j in range(i + 1, 4):
                g, h = grad[i], grad[j]
                block = [g[p] * h[p] for p in range(3)]
                block += [g[p] * h[q] + g[q] * h[p] for p, q in ((0, 1), (0, 2), (1, 2))]
                key = (path[i], path[j])
                blocks[key] = plus(blocks[key], block) if key in blocks else block
    for (v, _), block in blocks.items():
        trace = block[0] + block[1] + block[2]
        block[:3] = [same + same + trace for same in block[:3]]
        if v == (0, 0, 0):
            block[:] = [-w for w in block]

    def pick(mask, yes, no):
        return [jnp.where(mask, y, n) for y, n in zip(yes, no)]

    def keep(mask, values):
        return [jnp.where(mask, v, 0.0) for v in values]

    along_x = {(b, c): blocks[(0, b, c), (1, b, c)] for b in BITS for c in BITS}
    along_x = {(b, c): pick(flip_y, along_x[1 - b, c], along_x[b, c]) for b, c in along_x}
    along_x = {(b, c): pick(flip_z, along_x[b, 1 - c], along_x[b, c]) for b, c in along_x}
    along_y = {(a, c): blocks[(a, 0, c), (a, 1, c)] for a in BITS for c in BITS}
    along_y = {(a, c): pick(flip_z, along_y[a, 1 - c], along_y[a, c]) for a, c in along_y}
    along_z = {(a, b): blocks[(a, b, 0), (a, b, 1)] for a in BITS for b in BITS}
    along_z = {(a, b): pick(flip_y, along_z[a, 1 - b], along_z[a, b]) for a, b in along_z}
    no_y, no_z, unlike = ~flip_y, ~flip_z, flip_y ^ flip_z
    in_xy = [blocks[(0, 0, c), (1, 1, c)] for c in BITS]
    in_xy = [pick(flip_z, in_xy[1 - c], in_xy[c]) for c in BITS]
    in_xz = [blocks[(0, b, 0), (1, b, 1)] for b in BITS]
    in_xz = [pick(flip_y, in_xz[1 - b], in_xz[b]) for b in BITS]
    in_yz = [blocks[(a, 0, 0), (a, 1, 1)] for a in BITS]
    body = blocks[(0, 0, 0), top]
    return dict(
        x=along_x,
        y=along_y,
        z=along_z,
        xy=[(keep(no_y, v), keep(flip_y, v)) for v in in_xy],
        xz=[(keep(no_z, v), keep(flip_z, v)) for v in in_xz],
        yz=[(keep(~unlike, v), keep(unlike, v)) for v in in_yz],
        xyz={
            (0, 0): keep(no_y & no_z, body),
            (0, 1): keep(no_y & flip_z, body),
            (1, 0): keep(flip_y & no_z, body),
            (1, 1): keep(flip_y & flip_z, body),
        },
    )


def fill_rows(target_ref, rows_refs, odd, channel, to):
    own, swap1, swap2, swap3 = rows_refs
    for r in range(2):
        one, three = swap1[channel, r], swap3[channel, r]
        for place, value in (
            (0, own[channel, r]),
            (2, jnp.where(odd, three, one)),
            (4, swap2[channel, r]),
            (6, jnp.where(odd, one, three)),
        ):
            target_ref[to, :, place + r, :] = value


MOVING = ("z", "xz_up", "xz_down", "yz_up", "yz_down", "b00", "b01", "b10", "b11") + tuple(
    (name, c) for c in BITS for name in ("x", "y", "up", "down")
)


def node_parts(kinds):
    x, y, z = kinds["x"], kinds["y"], kinds["z"]
    (xz_up0, xz_down0), (xz_up1, xz_down1) = kinds["xz"]
    (yz_up0, yz_down0), (yz_up1, yz_down1) = kinds["yz"]
    body = {key: (v, back_y(v)) for key, v in kinds["xyz"].items()}
    moving = {
        "z": plus(z[1, 0], back_y(z[1, 1])),
        "xz_up": plus(xz_up0, back_y(xz_up1)),
        "xz_down": plus(xz_down0, back_y(xz_down1)),
        "yz_up": yz_up1,
        "yz_down": yz_down1,
        "b00": body[0, 0][1],
        "b01": body[0, 1][1],
        "b10": body[1, 0][0],
        "b11": body[1, 1][0],
    }
    still = {
        "z": plus(z[0, 0], back_y(z[0, 1])),
        "yz_up": yz_up0,
        "yz_down": yz_down0,
        "b00": body[0, 0][0],
        "b01": body[0, 1][0],
        "b10": body[1, 0][1],
        "b11": body[1, 1][1],
    }
    for c in BITS:
        up, down = kinds["xy"][c]
        moving["x", c] = plus(x[0, c], back_y(x[1, c]))
        moving["y", c] = y[1, c]
        moving["up", c] = back_y(up)
        moving["down", c] = down
        still["y", c] = y[0, c]
        still["up", c] = up
        still["down", c] = back_y(down)
    return moving, still


def setup_kernel(odd_ref, own_ref, swap1_ref, swap2_ref, swap3_ref, _, field_ref, side_ref):
    odd = odd_ref[0] == 1
    for c in range(5):
        fill_rows(field_ref, (own_ref, swap1_ref, swap2_ref, swap3_ref), odd, c, c)
    planes = field_ref.shape[1]
    gap = 128 // planes
    lane = lax.broadcasted_iota(I32, (8, 128), 1)

    packed = jnp.zeros((8, 128), F32)
    for k in range(planes):
        packed = jnp.where(lane // gap == k, pltpu.roll(field_ref[4, k], k * gap, 1), packed)
    corner = {}
    for a in BITS:
        for p in range(3):
            low = pltpu.roll(packed, 128 - (4 * a + p), 1) if a or p else packed
            for c, plane in ((0, low), (1, pltpu.roll(low, 128 - gap, 1))):
                corner.setdefault((a, 0, c), []).append(plane)
                corner.setdefault((a, 1, c), []).append(pltpu.roll(plane, 7, 0))
    moving, _ = node_parts(cell_blocks(corner, pltpu.roll(packed, 125, 1)))
    for m, name in enumerate(MOVING):
        for e in range(6):
            side_ref[m, e] = moving[name][e]


def setup(odd, rows, after):
    planes = rows[0].shape[2]
    return pl.pallas_call(
        setup_kernel,
        out_shape=(
            jax.ShapeDtypeStruct((5, planes, 8, 128), F32),
            jax.ShapeDtypeStruct((len(MOVING), 6, 8, 128), F32),
        ),
        in_specs=[SMEM] + [VMEM] * 5,
        out_specs=(VMEM,) * 2,
        compiler_params=params(4),
        cost_estimate=pl.CostEstimate(flops=SETUP_FLOPS, bytes_accessed=1000000, transcendentals=0),
        name="setup",
    )(odd, *rows, after)


def assemble_kernel(start, stop, field_ref, side_ref, coef_ref, step_ref):
    planes = field_ref.shape[1]
    gap = 128 // planes
    lane = lax.broadcasted_iota(I32, (8, 128), 1)
    first, last = lane == 0, lane == 127

    def cells(k, _):
        corner = {}
        for c in BITS:
            edge = field_ref[4, k + c]
            edges = (edge, pltpu.roll(edge, 7, 0))
            for p in range(3):
                low = field_ref[p, k + c]
                for b, row in ((0, low), (1, pltpu.roll(low, 7, 0))):
                    beyond = pltpu.roll(edges[b], 2 - p, 1) if p < 2 else edges[b]
                    corner.setdefault((0, b, c), []).append(row)
                    corner.setdefault((1, b, c), []).append(jnp.where(last, beyond, pltpu.roll(row, 127, 1)))
        moving, still = node_parts(cell_blocks(corner, field_ref[3, k]))
        shift = 128 - k * gap

        def back_x(name):
            m = MOVING.index(name)
            return [
                jnp.where(first, pltpu.roll(side_ref[m, e], shift, 1), pltpu.roll(moving[name][e], 1, 1))
                for e in range(6)
            ]

        def put(plane, step, values):
            for e in range(6):
                coef_ref[plane, SLOT_OF[step], e] = values[e]

        def add(plane, step, values):
            at = SLOT_OF[step]
            for e in range(6):
                coef_ref[plane, at, e] = coef_ref[plane, at, e] + values[e]

        low, high = k - start, k + 1 - start
        s = plus(still["z"], back_x("z"))
        put(low, (0, 0, 1), s)
        put(high, (0, 0, -1), s)
        put(low, (1, 0, 1), moving["xz_up"])
        put(high, (-1, 0, -1), back_x("xz_up"))
        put(high, (1, 0, -1), moving["xz_down"])
        put(low, (-1, 0, 1), back_x("xz_down"))
        s = plus(still["yz_up"], back_x("yz_up"))
        put(low, (0, 1, 1), s)
        put(high, (0, -1, -1), back_y(s))
        s = plus(still["yz_down"], back_x("yz_down"))
        put(high, (0, 1, -1), s)
        put(low, (0, -1, 1), back_y(s))
        put(low, (1, 1, 1), still["b00"])
        put(high, (-1, -1, -1), back_x("b00"))
        put(high, (1, 1, -1), still["b01"])
        put(low, (-1, -1, 1), back_x("b01"))
        put(low, (1, -1, 1), still["b10"])
        put(high, (-1, 1, -1), back_x("b10"))
        put(high, (1, -1, -1), still["b11"])
        put(low, (-1, 1, 1), back_x("b11"))
        for c, plane, store in ((0, low, add), (1, high, put)):
            store(plane, (1, 0, 0), moving["x", c])
            store(plane, (-1, 0, 0), back_x(("x", c)))
            s = plus(still["y", c], back_x(("y", c)))
            store(plane, (0, 1, 0), s)
            store(plane, (0, -1, 0), back_y(s))
            store(plane, (1, 1, 0), still["up", c])
            store(plane, (-1, -1, 0), back_x(("up", c)))
            store(plane, (1, -1, 0), still["down", c])
            store(plane, (-1, 1, 0), back_x(("down", c)))
        return 0

    lax.fori_loop(start, stop, cells, 0, unroll=8)

    def selves(k, _):
        for e in range(6):
            total = coef_ref[k, 0, e]
            for m in range(1, SELF):
                total = total + coef_ref[k, m, e]
            coef_ref[k, SELF, e] = -total
            if e < 3:
                step_ref[k, e] = -RELAX_FACTOR / total
        return 0

    lax.fori_loop(1, stop - start, selves, 0, unroll=7)


def assemble(field, side, start, stop):
    return pl.pallas_call(
        partial(assemble_kernel, start, stop),
        out_shape=(
            jax.ShapeDtypeStruct((stop - start + 1, SELF + 1, 6, 8, 128), F32),
            jax.ShapeDtypeStruct((stop - start + 1, 3, 8, 128), F32),
        ),
        in_specs=[VMEM] * 2,
        out_specs=(VMEM,) * 2,
        compiler_params=params(12),
        cost_estimate=pl.CostEstimate(
            flops=PLANE_FLOPS * (stop - start), bytes_accessed=1000000, transcendentals=0
        ),
        name="assemble",
    )(field, side)


def sweep_kernel(odd_ref, *refs):
    rows_refs = refs[:4]
    coef_a_ref, step_a_ref, coef_b_ref, step_b_ref, wall_ref, out_ref, motion_ref, edge_ref = refs[4:]
    odd = odd_ref[0] == 1
    planes = motion_ref.shape[1]
    middle = planes // 2
    for c in range(3):
        fill_rows(motion_ref, rows_refs, odd, c, c)
    fill_rows(edge_ref, rows_refs, odd, 3, 0)
    lane = lax.broadcasted_iota(I32, (8, 128), 1)
    first, last = lane == 0, lane == 127

    def neighbours(k):
        side = edge_ref[0, k]
        near = {}
        for c in range(3):
            here = motion_ref[c, k]
            before = pltpu.roll(side, 128 - c, 1) if c else side
            beyond = pltpu.roll(side, 2 - c, 1) if c < 2 else side
            for x, value in (
                (-1, jnp.where(first, before, pltpu.roll(here, 1, 1))),
                (0, here),
                (1, jnp.where(last, beyond, pltpu.roll(here, 127, 1))),
            ):
                near[c, 0, x] = value
                near[c, -1, x] = pltpu.roll(value, 1, 0)
                near[c, 1, x] = pltpu.roll(value, 7, 0)
        return near

    def reach(force, near, plane, z):
        coef_ref, at = (coef_a_ref, plane) if plane < middle else (coef_b_ref, plane - middle + 1)
        for y in (-1, 0, 1):
            for x in (-1, 0, 1):
                m = SLOT_OF.get((x, y, z), SELF)
                block = [coef_ref[at, m, e] for e in range(6)]
                for p in range(3):
                    term = sum(block[ENTRY[p][q]] * near[q, y, x] for q in range(3))
                    force[p] = term if force[p] is None else force[p] + term

    for sweep in range(SWEEPS):
        low, high = sweep + 1, planes - 2 - sweep
        force = {k: [None] * 3 for k in range(low, high + 1)}
        for k in range(low - 1, high + 2):
            near = neighbours(k)
            for z in (1, 0, -1):
                if low <= k - z <= high:
                    reach(force[k - z], near, k - z, z)
            done = k - 1
            if done in force:
                step_ref, at = (step_a_ref, done) if done < middle else (step_b_ref, done - middle + 1)
                for p in range(3):
                    motion_ref[p, done] = motion_ref[p, done] - step_ref[at, p] * force[done][p]
    for c in range(3):
        for y in range(2):
            out_ref[c, y, :, :128] = wall_ref[c, y]
            out_ref[c, y, :, 128:] = motion_ref[c, DEPTH : planes - DEPTH, y, :]


def sweeps(odd, rows, lower, upper, wall):
    planes = rows[0].shape[2]
    return pl.pallas_call(
        sweep_kernel,
        out_shape=jax.ShapeDtypeStruct((3, 2, planes - 2 * DEPTH, 256), F32),
        in_specs=[SMEM] + [VMEM] * 9,
        out_specs=VMEM,
        scratch_shapes=[
            pltpu.VMEM((3, planes, 8, 128), F32),
            pltpu.VMEM((1, planes, 8, 128), F32),
        ],
        compiler_params=params(20),
        name="sweeps",
    )(odd, *rows, *lower, *upper, wall)


def swap(block, partner):
    struct_count, fluid_count = lax.axis_size("struct"), lax.axis_size("fluid")
    route = []
    for s in range(struct_count):
        for f in range(fluid_count):
            to_s, to_f = partner(s, f)
            route.append((s * fluid_count + f, to_s * fluid_count + to_f % fluid_count))
    return lax.ppermute(block, BOTH, route)


def planes_apart(parts):
    _, for_pair, for_next = parts
    return (
        swap(for_pair, lambda s, f: (s, f ^ 1)),
        swap(for_next, lambda s, f: (s, ((f - 1) ^ 1) + 1)),
    )


def hold_kernel(whole_ref, out_ref):
    out_ref[...] = whole_ref[...]


def hold(whole):
    return pl.pallas_call(
        hold_kernel,
        out_shape=jax.ShapeDtypeStruct(whole.shape, F32),
        in_specs=[VMEM],
        out_specs=VMEM,
        compiler_params=params(4),
        cost_estimate=pl.CostEstimate(flops=2000000, bytes_accessed=1000000, transcendentals=0),
        name="hold",
    )(whole)


def widened(even, out_ref, to, whole, in_pair, next_pair):
    count = whole.shape[1]
    out_ref[to, :, :DEPTH] = jnp.where(even, next_pair, in_pair)
    out_ref[to, :, DEPTH : DEPTH + count] = whole
    out_ref[to, :, DEPTH + count :] = jnp.where(even, in_pair, next_pair)


def widen_fields_kernel(even_ref, whole_ref, pair_ref, next_ref, lattice_ref, prev_ref, plan_ref):
    even = even_ref[0] == 1
    for c in range(8):
        out_ref, to = (lattice_ref, c) if c < 5 else (prev_ref, c - 5)
        widened(even, out_ref, to, whole_ref[c], pair_ref[c], next_ref[c])
    plan_ref[...] = whole_ref[8:]


def widen_fields(even, whole, in_pair, next_pair):
    _, rows, count, lanes = whole.shape
    return pl.pallas_call(
        widen_fields_kernel,
        out_shape=(
            jax.ShapeDtypeStruct((5, rows, count + 2 * DEPTH, lanes), F32),
            jax.ShapeDtypeStruct((3, rows, count + 2 * DEPTH, lanes), F32),
            jax.ShapeDtypeStruct((8, rows, count, lanes), F32),
        ),
        in_specs=[SMEM] + [VMEM] * 3,
        out_specs=(VMEM,) * 3,
        compiler_params=params(4),
        name="widen_fields",
    )(even, whole, in_pair, next_pair)


def widen_wall_kernel(even_ref, prev_ref, columns_ref, pair_ref, next_ref, out_ref):
    out_ref[:3] = prev_ref[...]
    widened(even_ref[0] == 1, out_ref, 3, columns_ref[0], pair_ref[0], next_ref[0])


def widen_wall(even, prev, columns, in_pair, next_pair):
    return pl.pallas_call(
        widen_wall_kernel,
        out_shape=jax.ShapeDtypeStruct((4, *prev.shape[1:]), F32),
        in_specs=[SMEM] + [VMEM] * 4,
        out_specs=VMEM,
        compiler_params=params(4),
        name="widen_wall",
    )(even, prev, columns, in_pair, next_pair)


def all_rows(block):
    return [block] + [swap(block, lambda s, f, m=m: (s ^ m, f)) for m in (1, 2, 3)]


def shards(shell_motion, owner, stencil_slot, stencil_weight, prev_motion, node_offset, cell_split):
    odd = (lax.axis_index("struct") & 1).astype(I32).reshape(1)
    even = 1 - (lax.axis_index("fluid") & 1).astype(I32).reshape(1)
    packed, *sent = pack_and_fields(
        even, owner, shell_motion, node_offset, cell_split, prev_motion, stencil_slot, stencil_weight
    )
    apart = planes_apart(sent)
    whole = hold(sent[0])
    whole, *apart = lax.optimization_barrier((whole, *apart))
    lattice, prev, plan = widen_fields(even, whole, *apart)
    rows = all_rows(lattice)
    received = lax.all_to_all(packed, BOTH, split_axis=0, concat_axis=0, tiled=True)
    sent = wall_columns(even, received, plan)
    field, side = setup(odd, rows, sent[0])
    apart = planes_apart(sent)
    lower = assemble(field, side, 0, 8)
    lower, apart = lax.optimization_barrier((lower, apart))
    joined = widen_wall(even, prev, sent[0], *apart)
    field, side, received, joined = lax.optimization_barrier((field, side, received, joined))
    rows = all_rows(joined)
    upper = assemble(field, side, 7, 15)
    wall = gather(received, plan)
    return sweeps(odd, rows, lower, upper, wall)


def solution(mesh):
    return jax.shard_map(
        shards,
        mesh=mesh,
        in_specs=(
            P(None, BOTH),
            P(BOTH, None),
            P(None, "struct", "fluid", None),
            P(None, "struct", "fluid", None),
            P(None, "struct", "fluid", None),
            P(None, "struct", "fluid", None),
            P("struct", "fluid", None),
        ),
        out_specs=P(None, "struct", "fluid", None),
        check_vma=False,
    )
```

```python
from functools import partial

import jax
import jax.numpy as jnp
from jax import lax
from jax.experimental import pallas as pl
from jax.experimental.pallas import tpu as pltpu
from jax.sharding import PartitionSpec as P

SWEEPS = 4
RELAX_FACTOR = 0.5
STEP_ORDERS = ((0, 1, 2), (0, 2, 1), (1, 0, 2), (1, 2, 0), (2, 0, 1), (2, 1, 0))
BITS = (0, 1)
CORNERS = tuple((a, b, c) for a in BITS for b in BITS for c in BITS)
STEPS = tuple(
    (x, y, z) for z in (-1, 0, 1) for y in (-1, 0, 1) for x in (-1, 0, 1) if (x, y, z) != (0, 0, 0)
)
SLOT_OF = {step: k for k, step in enumerate(STEPS)}
SELF = len(STEPS)
ENTRY = ((0, 3, 4), (3, 1, 5), (4, 5, 2))
BOTH = ("struct", "fluid")
DEPTH = SWEEPS
SETUP_FLOPS, PLANE_FLOPS = 20000000, 20000000
FULL = 63
F32, BF16, I32 = jnp.float32, jnp.bfloat16, jnp.int32
VMEM = pl.BlockSpec(memory_space=pltpu.VMEM)
SMEM = pl.BlockSpec(memory_space=pltpu.SMEM)
HBM = pl.BlockSpec(memory_space=pltpu.HBM)


def fetch(sources, targets, semaphores):
    copies = [
        pltpu.make_async_copy(source, target, semaphores.at[k])
        for k, (source, target) in enumerate(zip(sources, targets))
    ]
    for copy in copies:
        copy.start()
    for copy in copies:
        copy.wait()


def params(mebibytes):
    return pltpu.CompilerParams(vmem_limit_bytes=int(mebibytes * 2**20))


def pack(owner_ref, value_ref, out_ref, left_ref, right_ref):
    count = owner_ref.shape[1]
    width = 256
    rows = lax.broadcasted_iota(I32, (width, width + 128), 0)
    columns = lax.broadcasted_iota(I32, (width, width + 128), 1)
    earlier = jnp.where((rows < columns) | (columns >= width), 1.0, 0.0).astype(BF16)
    owners = lax.broadcasted_iota(I32, (128, width), 0)
    pairs = lax.broadcasted_iota(I32, (64, width), 0)
    places = lax.broadcasted_iota(I32, (256, width), 0)
    base = jnp.zeros((128, 128), F32)
    for k in range(count // width):
        part = pl.ds(k * width, width)
        own = owner_ref[:, part]
        hit = owners == own
        before = jnp.dot(
            jnp.where(hit, 1.0, 0.0).astype(BF16), earlier, preferred_element_type=F32
        )
        running = before[:, :width] + jnp.concatenate([base, base], axis=1)
        rank = jnp.sum(jnp.where(hit, running, 0.0), axis=0, keepdims=True).astype(I32)
        base = base + before[:, width:]
        right_ref[:, part] = jnp.where(places == (own & 1) * 128 + rank, 1.0, 0.0).astype(BF16)
        half = pairs == (own >> 1)
        for c in range(3):
            value = value_ref[c : c + 1, part]
            high = value.astype(BF16).astype(F32)
            low = value - high
            left_ref[c * 64 : c * 64 + 64, part] = jnp.where(half, high, 0.0).astype(BF16)
            left_ref[192 + c * 64 : 256 + c * 64, part] = jnp.where(half, low, 0.0).astype(BF16)
    product = lax.dot_general(
        left_ref[...], right_ref[...], (((1,), (1,)), ((), ())), preferred_element_type=F32
    )
    both = product[:192] + product[192:]
    for c in range(3):
        for h in range(2):
            out_ref[pl.ds(h, 64, stride=2), c, :] = both[c * 64 : c * 64 + 64, h * 128 : h * 128 + 128]


def payload(kept, sent):
    return (
        jax.ShapeDtypeStruct((kept, 2, 8, 128), F32),
        jax.ShapeDtypeStruct((sent, 2, DEPTH, 128), F32),
        jax.ShapeDtypeStruct((sent, 2, DEPTH, 128), F32),
    )


def emit(refs, even, channel, y, value):
    whole_ref, pair_ref, next_ref = refs
    first, last = value[:DEPTH], value[DEPTH:]
    whole_ref[channel, y] = value
    pair_ref[channel, y] = jnp.where(even, last, first)
    next_ref[channel, y] = jnp.where(even, first, last)


def fields(even, offset_ref, split_ref, prev_ref, slot_ref, weight_ref, out_refs):
    out_refs[0][8:12] = slot_ref[...].astype(F32)
    out_refs[0][12:16] = weight_ref[...]
    lane = lax.broadcasted_iota(I32, (8, 128), 1)
    for y in range(2):
        code = split_ref[y].astype(F32)
        columns = jnp.where(lane == 3, pltpu.roll(code[:, :128], 4, 1), 0.0)
        for p in range(3):
            wall, free = offset_ref[p, y, :, :128], offset_ref[p, y, :, 128:]
            columns = jnp.where(lane == p, pltpu.roll(wall, p + 1, 1), columns)
            columns = jnp.where(lane == 4 + p, pltpu.roll(free, 4 + p, 1), columns)
            columns = jnp.where(lane == 125 + p, pltpu.roll(wall, 125 + p, 1), columns)
            emit(out_refs, even, p, y, free)
            emit(out_refs, even, 5 + p, y, prev_ref[p, y, :, 128:])
        emit(out_refs, even, 3, y, code[:, 128:])
        emit(out_refs, even, 4, y, columns)


def first_kernel(even_ref, *refs):
    sources, outs, inputs = refs[:7], refs[7:11], refs[11:18]
    left_ref, right_ref, semaphores = refs[18:]
    fetch(sources, inputs, semaphores)
    fields(even_ref[0] == 1, *inputs[2:], outs[1:])
    pack(*inputs[:2], outs[0], left_ref, right_ref)


def pack_and_fields(even, owner, *others):
    count = owner.shape[0]
    inputs = (owner.reshape(1, count), *others)
    return pl.pallas_call(
        first_kernel,
        out_shape=(jax.ShapeDtypeStruct((128, 3, 128), F32), *payload(16, 8)),
        in_specs=[SMEM] + [HBM] * 7,
        out_specs=(VMEM,) * 4,
        scratch_shapes=[
            *(pltpu.VMEM(x.shape, x.dtype) for x in inputs),
            pltpu.VMEM((384, count), BF16),
            pltpu.VMEM((256, count), BF16),
            pltpu.SemaphoreType.DMA((7,)),
        ],
        compiler_params=params(FULL),
        name="first",
    )(even, *inputs)


def columns_kernel(even_ref, received_ref, plan_ref, *refs):
    column_refs, table_ref = refs[:3], refs[3]
    for c in range(3):
        flat = received_ref[:, c, :]
        high = flat.astype(BF16).astype(F32)
        low = flat - high
        for part, base in ((high, 0), (low, 192)):
            at = slice(base + c * 64, base + c * 64 + 64)
            table_ref[:128, at] = part[:, :64].astype(BF16)
            table_ref[128:, at] = part[:, 64:].astype(BF16)

    def stacked(first):
        return jnp.concatenate(
            [
                plan_ref[first + t, y, :, x : x + 1]
                for t in range(4)
                for y in range(2)
                for x in (127, 0)
            ]
        )

    slot = stacked(0).astype(I32)
    weight = stacked(4)
    pick = ((slot >> 6) & 1) * 128 + (slot >> 7)
    hot = jnp.where(lax.broadcasted_iota(I32, (128, 256), 1) == pick, 1.0, 0.0).astype(BF16)
    found = jnp.dot(hot, table_ref[...], preferred_element_type=F32)
    found = found[:, :192] + found[:, 192:]
    share = jnp.where(lax.broadcasted_iota(I32, (128, 192), 1) % 64 == (slot & 63), weight, 0.0) * found
    share = share[:32] + share[32:64] + share[64:96] + share[96:]
    values = [jnp.sum(share[:, c * 64 : c * 64 + 64], axis=1, keepdims=True) for c in range(3)]
    lane = lax.broadcasted_iota(I32, (8, 128), 1)
    for y in range(2):
        columns = jnp.zeros((8, 128), F32)
        for c in range(3):
            columns = jnp.where(lane == c, values[c][y * 16 : y * 16 + 8], columns)
            columns = jnp.where(lane == 125 + c, values[c][y * 16 + 8 : y * 16 + 16], columns)
        emit(column_refs, even_ref[0] == 1, 0, y, columns)


def wall_columns(even, received, plan):
    return pl.pallas_call(
        columns_kernel,
        out_shape=payload(1, 1),
        in_specs=[SMEM] + [VMEM] * 2,
        out_specs=(VMEM,) * 3,
        scratch_shapes=[pltpu.VMEM((256, 384), BF16)],
        compiler_params=params(8),
        name="columns",
    )(even, received, plan)


def gather_kernel(received_ref, plan_ref, out_ref, table_ref):
    for c in range(3):
        flat = received_ref[:, c, :].T
        high = flat.astype(BF16).astype(F32)
        low = flat - high
        for part, base in ((high, 0), (low, 192)):
            at = base + c * 64
            table_ref[at : at + 64, :128] = part[:64].astype(BF16)
            table_ref[at : at + 64, 128:] = part[64:].astype(BF16)
    table = table_ref[...]
    picks = lax.broadcasted_iota(I32, (256, 256), 0)
    places = lax.broadcasted_iota(I32, (64, 256), 0)
    for y in range(2):
        for z in range(0, 8, 2):
            total = [jnp.zeros((64, 256), F32) for _ in range(3)]
            for t in range(4):
                slot, weight = [
                    jnp.concatenate([plan_ref[first + t, y, z + k : z + k + 1, :] for k in BITS], axis=1)
                    for first in (0, 4)
                ]
                slot = slot.astype(I32)
                pick = ((slot >> 6) & 1) * 128 + (slot >> 7)
                hot = jnp.where(picks == pick, 1.0, 0.0).astype(BF16)
                found = jnp.dot(table, hot, preferred_element_type=F32)
                share = jnp.where(places == (slot & 63), weight, 0.0)
                for c in range(3):
                    at = c * 64
                    total[c] = total[c] + share * (found[at : at + 64] + found[at + 192 : at + 256])
            for c in range(3):
                line = jnp.sum(total[c], axis=0, keepdims=True)
                for k in BITS:
                    out_ref[c, y, z + k : z + k + 1, :] = line[:, k * 128 : k * 128 + 128]


def gather(received, plan):
    return pl.pallas_call(
        gather_kernel,
        out_shape=jax.ShapeDtypeStruct((3, 2, 8, 128), F32),
        in_specs=[VMEM] * 2,
        out_specs=VMEM,
        scratch_shapes=[pltpu.VMEM((384, 256), BF16)],
        compiler_params=params(8),
        cost_estimate=pl.CostEstimate(flops=60000000, bytes_accessed=1000000, transcendentals=0),
        name="gather",
    )(received, plan)


def back_y(values):
    return [pltpu.roll(v, 1, 0) for v in values]


def plus(u, v):
    return [p + q for p, q in zip(u, v)]


def cross(u, v):
    return [
        u[1] * v[2] - u[2] * v[1],
        u[2] * v[0] - u[0] * v[2],
        u[0] * v[1] - u[1] * v[0],
    ]


def cell_gradients(corner, code):
    flip_y = code >= 2
    flip_z = (code == 1) | (code == 3)
    sign_y = jnp.where(flip_y, -1.0, 1.0)
    sign_z = jnp.where(flip_z, -1.0, 1.0)
    named = {}
    for a, b, c in CORNERS:
        named[a, b, c] = [jnp.where(flip_y, corner[a, 1 - b, c][p], corner[a, b, c][p]) for p in range(3)]
    named = {
        (a, b, c): [jnp.where(flip_z, named[a, b, 1 - c][p], named[a, b, c][p]) for p in range(3)]
        for a, b, c in CORNERS
    }
    edge = {}
    for v in CORNERS[1:]:
        moved = [named[v][p] - named[0, 0, 0][p] for p in range(3)]
        if v[0]:
            moved[0] = moved[0] + 1.0
        if v[1]:
            moved[1] = moved[1] + sign_y
        if v[2]:
            moved[2] = moved[2] + sign_z
        edge[v] = moved
    top = (1, 1, 1)
    over = {v: cross(edge[v], edge[top]) for v in CORNERS[1:-1]}
    tetrahedra = []
    for order in STEP_ORDERS:
        at = [0, 0, 0]
        path = [(0, 0, 0)]
        for axis in order:
            at[axis] = 1
            path.append(tuple(at))
        one, two = path[1], path[2]
        third = cross(edge[one], edge[two])
        volume = sum(edge[one][p] * over[two][p] for p in range(3))
        inverse = 1.0 / volume
        minus = -inverse
        grad = [None, [w * inverse for w in over[two]], [w * minus for w in over[one]], [w * inverse for w in third]]
        grad[0] = [grad[1][p] + grad[2][p] + grad[3][p] for p in range(3)]
        tetrahedra.append((path, grad))
    return (flip_y, flip_z), tetrahedra


def edge_products(tetrahedra, p, q):
    sums = {}
    for path, grad in tetrahedra:
        for i in range(4):
            for j in range(i + 1, 4):
                g, h = grad[i], grad[j]
                product = g[p] * h[p] if p == q else g[p] * h[q] + g[q] * h[p]
                key = (path[i], path[j])
                sums[key] = sums[key] + product if key in sums else product
    return sums


def edge_entries(tetrahedra):
    squares = [edge_products(tetrahedra, p, p) for p in range(3)]
    trace = {key: squares[0][key] + squares[1][key] + squares[2][key] for key in squares[0]}
    for e, (p, q) in enumerate(((0, 0), (1, 1), (2, 2), (0, 1), (0, 2), (1, 2))):
        if p == q:
            values = {key: v + v + trace[key] for key, v in squares[p].items()}
        else:
            values = edge_products(tetrahedra, p, q)
        yield e, {key: [-v if key[0] == (0, 0, 0) else v] for key, v in values.items()}


def cell_kinds(blocks, flips):
    flip_y, flip_z = flips
    top = (1, 1, 1)

    def pick(mask, yes, no):
        return [jnp.where(mask, y, n) for y, n in zip(yes, no)]

    def keep(mask, values):
        return [jnp.where(mask, v, 0.0) for v in values]

    along_x = {(b, c): blocks[(0, b, c), (1, b, c)] for b in BITS for c in BITS}
    along_x = {(b, c): pick(flip_y, along_x[1 - b, c], along_x[b, c]) for b, c in along_x}
    along_x = {(b, c): pick(flip_z, along_x[b, 1 - c], along_x[b, c]) for b, c in along_x}
    along_y = {(a, c): blocks[(a, 0, c), (a, 1, c)] for a in BITS for c in BITS}
    along_y = {(a, c): pick(flip_z, along_y[a, 1 - c], along_y[a, c]) for a, c in along_y}
    along_z = {(a, b): blocks[(a, b, 0), (a, b, 1)] for a in BITS for b in BITS}
    along_z = {(a, b): pick(flip_y, along_z[a, 1 - b], along_z[a, b]) for a, b in along_z}
    no_y, no_z, unlike = ~flip_y, ~flip_z, flip_y ^ flip_z
    in_xy = [blocks[(0, 0, c), (1, 1, c)] for c in BITS]
    in_xy = [pick(flip_z, in_xy[1 - c], in_xy[c]) for c in BITS]
    in_xz = [blocks[(0, b, 0), (1, b, 1)] for b in BITS]
    in_xz = [pick(flip_y, in_xz[1 - b], in_xz[b]) for b in BITS]
    in_yz = [blocks[(a, 0, 0), (a, 1, 1)] for a in BITS]
    body = blocks[(0, 0, 0), top]
    return dict(
        x=along_x,
        y=along_y,
        z=along_z,
        xy=[(keep(no_y, v), keep(flip_y, v)) for v in in_xy],
        xz=[(keep(no_z, v), keep(flip_z, v)) for v in in_xz],
        yz=[(keep(~unlike, v), keep(unlike, v)) for v in in_yz],
        xyz={
            (0, 0): keep(no_y & no_z, body),
            (0, 1): keep(no_y & flip_z, body),
            (1, 0): keep(flip_y & no_z, body),
            (1, 1): keep(flip_y & flip_z, body),
        },
    )


def fill_rows(target_ref, rows_refs, odd, channel, to):
    own, swap1, swap2, swap3 = rows_refs
    for r in range(2):
        one, three = swap1[channel, r], swap3[channel, r]
        for place, value in (
            (0, own[channel, r]),
            (2, jnp.where(odd, three, one)),
            (4, swap2[channel, r]),
            (6, jnp.where(odd, one, three)),
        ):
            target_ref[to, :, place + r, :] = value


MOVING = ("z", "xz_up", "xz_down", "yz_up", "yz_down", "b00", "b01", "b10", "b11") + tuple(
    (name, c) for c in BITS for name in ("x", "y", "up", "down")
)


def node_parts(kinds):
    x, y, z = kinds["x"], kinds["y"], kinds["z"]
    (xz_up0, xz_down0), (xz_up1, xz_down1) = kinds["xz"]
    (yz_up0, yz_down0), (yz_up1, yz_down1) = kinds["yz"]
    body = {key: (v, back_y(v)) for key, v in kinds["xyz"].items()}
    moving = {
        "z": plus(z[1, 0], back_y(z[1, 1])),
        "xz_up": plus(xz_up0, back_y(xz_up1)),
        "xz_down": plus(xz_down0, back_y(xz_down1)),
        "yz_up": yz_up1,
        "yz_down": yz_down1,
        "b00": body[0, 0][1],
        "b01": body[0, 1][1],
        "b10": body[1, 0][0],
        "b11": body[1, 1][0],
    }
    still = {
        "z": plus(z[0, 0], back_y(z[0, 1])),
        "yz_up": yz_up0,
        "yz_down": yz_down0,
        "b00": body[0, 0][0],
        "b01": body[0, 1][0],
        "b10": body[1, 0][1],
        "b11": body[1, 1][1],
    }
    for c in BITS:
        up, down = kinds["xy"][c]
        moving["x", c] = plus(x[0, c], back_y(x[1, c]))
        moving["y", c] = y[1, c]
        moving["up", c] = back_y(up)
        moving["down", c] = down
        still["y", c] = y[0, c]
        still["up", c] = up
        still["down", c] = back_y(down)
    return moving, still


def setup_kernel(odd_ref, own_ref, swap1_ref, swap2_ref, swap3_ref, _, field_ref, side_ref):
    odd = odd_ref[0] == 1
    for c in range(5):
        fill_rows(field_ref, (own_ref, swap1_ref, swap2_ref, swap3_ref), odd, c, c)
    planes = field_ref.shape[1]
    gap = 128 // planes
    lane = lax.broadcasted_iota(I32, (8, 128), 1)

    packed = jnp.zeros((8, 128), F32)
    for k in range(planes):
        packed = jnp.where(lane // gap == k, pltpu.roll(field_ref[4, k], k * gap, 1), packed)
    corner = {}
    for a in BITS:
        for p in range(3):
            low = pltpu.roll(packed, 128 - (4 * a + p), 1) if a or p else packed
            for c, plane in ((0, low), (1, pltpu.roll(low, 128 - gap, 1))):
                corner.setdefault((a, 0, c), []).append(plane)
                corner.setdefault((a, 1, c), []).append(pltpu.roll(plane, 7, 0))
    flips, tetrahedra = cell_gradients(corner, pltpu.roll(packed, 125, 1))
    for e, blocks in edge_entries(tetrahedra):
        moving, _ = node_parts(cell_kinds(blocks, flips))
        for m, name in enumerate(MOVING):
            side_ref[m, e] = moving[name][0]


def setup(odd, rows, after):
    planes = rows[0].shape[2]
    return pl.pallas_call(
        setup_kernel,
        out_shape=(
            jax.ShapeDtypeStruct((5, planes, 8, 128), F32),
            jax.ShapeDtypeStruct((len(MOVING), 6, 8, 128), F32),
        ),
        in_specs=[SMEM] + [VMEM] * 5,
        out_specs=(VMEM,) * 2,
        compiler_params=params(4),
        cost_estimate=pl.CostEstimate(flops=SETUP_FLOPS, bytes_accessed=1000000, transcendentals=0),
        name="setup",
    )(odd, *rows, after)


def assemble_kernel(start, stop, field_ref, side_ref, coef_ref, step_ref):
    planes = field_ref.shape[1]
    gap = 128 // planes
    lane = lax.broadcasted_iota(I32, (8, 128), 1)
    first, last = lane == 0, lane == 127

    def scatter(k, e, moving, still):
        shift = 128 - k * gap

        def back_x(name):
            m = MOVING.index(name)
            return [jnp.where(first, pltpu.roll(side_ref[m, e], shift, 1), pltpu.roll(moving[name][0], 1, 1))]

        def put(plane, step, values):
            coef_ref[plane, SLOT_OF[step], e] = values[0]

        def add(plane, step, values):
            at = SLOT_OF[step]
            coef_ref[plane, at, e] = coef_ref[plane, at, e] + values[0]

        low, high = k - start, k + 1 - start
        s = plus(still["z"], back_x("z"))
        put(low, (0, 0, 1), s)
        put(high, (0, 0, -1), s)
        put(low, (1, 0, 1), moving["xz_up"])
        put(high, (-1, 0, -1), back_x("xz_up"))
        put(high, (1, 0, -1), moving["xz_down"])
        put(low, (-1, 0, 1), back_x("xz_down"))
        s = plus(still["yz_up"], back_x("yz_up"))
        put(low, (0, 1, 1), s)
        put(high, (0, -1, -1), back_y(s))
        s = plus(still["yz_down"], back_x("yz_down"))
        put(high, (0, 1, -1), s)
        put(low, (0, -1, 1), back_y(s))
        put(low, (1, 1, 1), still["b00"])
        put(high, (-1, -1, -1), back_x("b00"))
        put(high, (1, 1, -1), still["b01"])
        put(low, (-1, -1, 1), back_x("b01"))
        put(low, (1, -1, 1), still["b10"])
        put(high, (-1, 1, -1), back_x("b10"))
        put(high, (1, -1, -1), still["b11"])
        put(low, (-1, 1, 1), back_x("b11"))
        for c, plane, store in ((0, low, add), (1, high, put)):
            store(plane, (1, 0, 0), moving["x", c])
            store(plane, (-1, 0, 0), back_x(("x", c)))
            s = plus(still["y", c], back_x(("y", c)))
            store(plane, (0, 1, 0), s)
            store(plane, (0, -1, 0), back_y(s))
            store(plane, (1, 1, 0), still["up", c])
            store(plane, (-1, -1, 0), back_x(("up", c)))
            store(plane, (1, -1, 0), still["down", c])
            store(plane, (-1, 1, 0), back_x(("down", c)))

    def cells(k, _):
        corner = {}
        for c in BITS:
            edge = field_ref[4, k + c]
            edges = (edge, pltpu.roll(edge, 7, 0))
            for p in range(3):
                low = field_ref[p, k + c]
                for b, row in ((0, low), (1, pltpu.roll(low, 7, 0))):
                    beyond = pltpu.roll(edges[b], 2 - p, 1) if p < 2 else edges[b]
                    corner.setdefault((0, b, c), []).append(row)
                    corner.setdefault((1, b, c), []).append(jnp.where(last, beyond, pltpu.roll(row, 127, 1)))
        flips, tetrahedra = cell_gradients(corner, field_ref[3, k])
        for e, blocks in edge_entries(tetrahedra):
            scatter(k, e, *node_parts(cell_kinds(blocks, flips)))
        return 0

    lax.fori_loop(start, stop, cells, 0, unroll=8)

    def selves(k, _):
        for e in range(6):
            total = coef_ref[k, 0, e]
            for m in range(1, SELF):
                total = total + coef_ref[k, m, e]
            coef_ref[k, SELF, e] = -total
            if e < 3:
                step_ref[k, e] = -RELAX_FACTOR / total
        return 0

    lax.fori_loop(1, stop - start, selves, 0, unroll=7)


def assemble(field, side, start, stop):
    return pl.pallas_call(
        partial(assemble_kernel, start, stop),
        out_shape=(
            jax.ShapeDtypeStruct((stop - start + 1, SELF + 1, 6, 8, 128), F32),
            jax.ShapeDtypeStruct((stop - start + 1, 3, 8, 128), F32),
        ),
        in_specs=[VMEM] * 2,
        out_specs=(VMEM,) * 2,
        compiler_params=params(12),
        cost_estimate=pl.CostEstimate(
            flops=PLANE_FLOPS * (stop - start), bytes_accessed=1000000, transcendentals=0
        ),
        name="assemble",
    )(field, side)


def sweep_kernel(odd_ref, *refs):
    rows_refs = refs[:4]
    coef_a_ref, step_a_ref, coef_b_ref, step_b_ref, wall_ref, out_ref, motion_ref, edge_ref = refs[4:]
    odd = odd_ref[0] == 1
    planes = motion_ref.shape[1]
    middle = planes // 2
    for c in range(3):
        fill_rows(motion_ref, rows_refs, odd, c, c)
    fill_rows(edge_ref, rows_refs, odd, 3, 0)
    lane = lax.broadcasted_iota(I32, (8, 128), 1)
    first, last = lane == 0, lane == 127

    def neighbours(k):
        side = edge_ref[0, k]
        near = {}
        for c in range(3):
            here = motion_ref[c, k]
            before = pltpu.roll(side, 128 - c, 1) if c else side
            beyond = pltpu.roll(side, 2 - c, 1) if c < 2 else side
            for x, value in (
                (-1, jnp.where(first, before, pltpu.roll(here, 1, 1))),
                (0, here),
                (1, jnp.where(last, beyond, pltpu.roll(here, 127, 1))),
            ):
                near[c, 0, x] = value
                near[c, -1, x] = pltpu.roll(value, 1, 0)
                near[c, 1, x] = pltpu.roll(value, 7, 0)
        return near

    def reach(force, near, plane, z):
        coef_ref, at = (coef_a_ref, plane) if plane < middle else (coef_b_ref, plane - middle + 1)
        for y in (-1, 0, 1):
            for x in (-1, 0, 1):
                m = SLOT_OF.get((x, y, z), SELF)
                block = [coef_ref[at, m, e] for e in range(6)]
                for p in range(3):
                    term = sum(block[ENTRY[p][q]] * near[q, y, x] for q in range(3))
                    force[p] = term if force[p] is None else force[p] + term

    for sweep in range(SWEEPS):
        low, high = sweep + 1, planes - 2 - sweep
        force = {k: [None] * 3 for k in range(low, high + 1)}
        for k in range(low - 1, high + 2):
            near = neighbours(k)
            for z in (1, 0, -1):
                if low <= k - z <= high:
                    reach(force[k - z], near, k - z, z)
            done = k - 1
            if done in force:
                step_ref, at = (step_a_ref, done) if done < middle else (step_b_ref, done - middle + 1)
                for p in range(3):
                    motion_ref[p, done] = motion_ref[p, done] - step_ref[at, p] * force[done][p]
    for c in range(3):
        for y in range(2):
            out_ref[c, y, :, :128] = wall_ref[c, y]
            out_ref[c, y, :, 128:] = motion_ref[c, DEPTH : planes - DEPTH, y, :]


def sweeps(odd, rows, lower, upper, wall):
    planes = rows[0].shape[2]
    return pl.pallas_call(
        sweep_kernel,
        out_shape=jax.ShapeDtypeStruct((3, 2, planes - 2 * DEPTH, 256), F32),
        in_specs=[SMEM] + [VMEM] * 9,
        out_specs=VMEM,
        scratch_shapes=[
            pltpu.VMEM((3, planes, 8, 128), F32),
            pltpu.VMEM((1, planes, 8, 128), F32),
        ],
        compiler_params=params(20),
        name="sweeps",
    )(odd, *rows, *lower, *upper, wall)


def swap(block, partner):
    struct_count, fluid_count = lax.axis_size("struct"), lax.axis_size("fluid")
    route = []
    for s in range(struct_count):
        for f in range(fluid_count):
            to_s, to_f = partner(s, f)
            route.append((s * fluid_count + f, to_s * fluid_count + to_f % fluid_count))
    return lax.ppermute(block, BOTH, route)


def planes_apart(parts):
    _, for_pair, for_next = parts
    return (
        swap(for_pair, lambda s, f: (s, f ^ 1)),
        swap(for_next, lambda s, f: (s, ((f - 1) ^ 1) + 1)),
    )


def hold_kernel(whole_ref, out_ref):
    out_ref[...] = whole_ref[...]


def hold(whole):
    return pl.pallas_call(
        hold_kernel,
        out_shape=jax.ShapeDtypeStruct(whole.shape, F32),
        in_specs=[VMEM],
        out_specs=VMEM,
        compiler_params=params(4),
        cost_estimate=pl.CostEstimate(flops=2000000, bytes_accessed=1000000, transcendentals=0),
        name="hold",
    )(whole)


def widened(even, out_ref, to, whole, in_pair, next_pair):
    count = whole.shape[1]
    out_ref[to, :, :DEPTH] = jnp.where(even, next_pair, in_pair)
    out_ref[to, :, DEPTH : DEPTH + count] = whole
    out_ref[to, :, DEPTH + count :] = jnp.where(even, in_pair, next_pair)


def widen_fields_kernel(even_ref, whole_ref, pair_ref, next_ref, lattice_ref, prev_ref, plan_ref):
    even = even_ref[0] == 1
    for c in range(8):
        out_ref, to = (lattice_ref, c) if c < 5 else (prev_ref, c - 5)
        widened(even, out_ref, to, whole_ref[c], pair_ref[c], next_ref[c])
    plan_ref[...] = whole_ref[8:]


def widen_fields(even, whole, in_pair, next_pair):
    _, rows, count, lanes = whole.shape
    return pl.pallas_call(
        widen_fields_kernel,
        out_shape=(
            jax.ShapeDtypeStruct((5, rows, count + 2 * DEPTH, lanes), F32),
            jax.ShapeDtypeStruct((3, rows, count + 2 * DEPTH, lanes), F32),
            jax.ShapeDtypeStruct((8, rows, count, lanes), F32),
        ),
        in_specs=[SMEM] + [VMEM] * 3,
        out_specs=(VMEM,) * 3,
        compiler_params=params(4),
        name="widen_fields",
    )(even, whole, in_pair, next_pair)


def widen_wall_kernel(even_ref, prev_ref, columns_ref, pair_ref, next_ref, out_ref):
    out_ref[:3] = prev_ref[...]
    widened(even_ref[0] == 1, out_ref, 3, columns_ref[0], pair_ref[0], next_ref[0])


def widen_wall(even, prev, columns, in_pair, next_pair):
    return pl.pallas_call(
        widen_wall_kernel,
        out_shape=jax.ShapeDtypeStruct((4, *prev.shape[1:]), F32),
        in_specs=[SMEM] + [VMEM] * 4,
        out_specs=VMEM,
        compiler_params=params(4),
        name="widen_wall",
    )(even, prev, columns, in_pair, next_pair)


def all_rows(block):
    return [block] + [swap(block, lambda s, f, m=m: (s ^ m, f)) for m in (1, 2, 3)]


def shards(shell_motion, owner, stencil_slot, stencil_weight, prev_motion, node_offset, cell_split):
    odd = (lax.axis_index("struct") & 1).astype(I32).reshape(1)
    even = 1 - (lax.axis_index("fluid") & 1).astype(I32).reshape(1)
    packed, *sent = pack_and_fields(
        even, owner, shell_motion, node_offset, cell_split, prev_motion, stencil_slot, stencil_weight
    )
    apart = planes_apart(sent)
    whole = hold(sent[0])
    whole, *apart = lax.optimization_barrier((whole, *apart))
    lattice, prev, plan = widen_fields(even, whole, *apart)
    rows = all_rows(lattice)
    received = lax.all_to_all(packed, BOTH, split_axis=0, concat_axis=0, tiled=True)
    sent = wall_columns(even, received, plan)
    field, side = setup(odd, rows, sent[0])
    apart = planes_apart(sent)
    lower = assemble(field, side, 0, 8)
    lower, apart = lax.optimization_barrier((lower, apart))
    joined = widen_wall(even, prev, sent[0], *apart)
    field, side, received, joined = lax.optimization_barrier((field, side, received, joined))
    rows = all_rows(joined)
    upper = assemble(field, side, 7, 15)
    wall = gather(received, plan)
    return sweeps(odd, rows, lower, upper, wall)


def solution(mesh):
    return jax.shard_map(
        shards,
        mesh=mesh,
        in_specs=(
            P(None, BOTH),
            P(BOTH, None),
            P(None, "struct", "fluid", None),
            P(None, "struct", "fluid", None),
            P(None, "struct", "fluid", None),
            P(None, "struct", "fluid", None),
            P("struct", "fluid", None),
        ),
        out_specs=P(None, "struct", "fluid", None),
        check_vma=False,
    )
```
